32 devices in a mesh: grp: 8 (over y, x, core), aux: 4 (over z).
Axes of the slice: x: 2, y: 2, z: 4, core: 2. Of those that a mesh axis runs over, the one named last changes fastest.
Arguments:
- integral_tiles: bfloat16 [8, 4, 12, 32, 128, 128], P('grp', 'aux'), may hold values from -6 to 6
- row_blocks: int32 [8, 4, 12], P('grp', 'aux'), may hold values from 0 to 31
- col_blocks: int32 [8, 4, 12], P('grp', 'aux'), may hold values from 0 to 3
- aux_blocks: int32 [8, 4, 12], P('grp', 'aux'), may hold values from 0 to 15
- tile_counts: int32 [8, 4], P('grp', 'aux'), may hold values from 1 to 12, as said below
- occ_coeffs: bfloat16 [8, 4096], P(None, 'grp'), may hold values from -0.5 to 0.5
- vir_coeffs: bfloat16 [4096, 1024], P('grp'), may hold values from -0.5 to 0.5
Outputs:
- pair_factors: float32 [8192, 2048], P(('grp', 'aux'))
The draws below stay inside these ranges and needn't reach their ends.
Inputs may be any that keep to these rules, and one draw needn't show every extreme that they name: `tile_counts`: tile counts of the devices; some device holds exactly 12 kept tiles.
All inputs are finite; a program needn't handle non-finite values.
Results may differ from the reference program's by a relative error of at most 0.0029.
Values may be sent and summed in bfloat16 or wider, within the bound.
No kernel may reach another device: no remote copies, remote signals or barrier semaphores. Data moves between devices by JAX's collectives and lax.ppermute only.
A program may use at most 128 MiB of HBM per device.

```python
import jax
import jax.numpy as jnp
from jax import lax

O = 8
V = 1024
BLK = 128
PB = 32
NBG = 4
PDEV = 512
KMAX = 12
NAO = 4096
NAUX = 2048
N_GRP = 8
N_AUX = 4


def draw_tile_counts(key, part):
    first_key, second_key = jax.random.split(jax.random.fold_in(key, 7))
    base = jax.random.randint(first_key, (N_GRP * N_AUX,), 1, KMAX + 1)
    chosen = jax.random.randint(second_key, (), 0, N_GRP * N_AUX)
    filled = jnp.where(jnp.arange(N_GRP * N_AUX) == chosen, KMAX, base)
    return filled.reshape(N_GRP, N_AUX).astype(jnp.int32)


def set_ends(entries, own_key, least, top_value):
    shape = entries.shape
    index_at = [jax.random.randint(jax.random.fold_in(own_key, axis), (), 0, shape[axis]) for axis in range(len(shape))]
    entries = entries.at[tuple(index_at)].set(least)
    longest = shape.index(max(shape))
    index_at[longest] = (index_at[longest] + 1) % shape[longest]
    return entries.at[tuple(index_at)].set(top_value)


def shard_levels(rng, extent, pieces, low, high):
    factor_of = 1.0
    for position, parts in pieces:
        draws = jax.random.uniform(jax.random.fold_in(jax.random.fold_in(rng, 6), position), (parts,), jnp.float32, low / len(pieces), high / len(pieces))
        factor_of = factor_of * jnp.repeat(jnp.exp(draws), extent[position] // parts).reshape((-1,) + (1,) * (len(extent) - 1 - position))
    return factor_of


def centred(stream_key, shape, width, most, pieces=(), held_as=jnp.bfloat16):
    loudness = shard_levels(stream_key, shape, pieces, -0.22, 0.18) if pieces else 1.0
    drawn = jax.random.normal(stream_key, shape, jnp.float32) * width * loudness
    return jnp.minimum(jnp.maximum(drawn, -most), most).astype(held_as)


def setup_inputs(seed: int = 0) -> dict:
    arg_keys = jax.random.split(jax.random.key(seed), 8)
    return {
        "integral_tiles": centred(arg_keys[0], (N_GRP, N_AUX, KMAX, PB, BLK, BLK), 1.0, 6.0, ((0, 8), (1, 4))),
        "row_blocks": set_ends(jax.random.randint(arg_keys[1], (N_GRP, N_AUX, KMAX), 0, NBG * N_GRP), jax.random.fold_in(arg_keys[1], 1), 0, (NBG * N_GRP) - 1).astype(jnp.int32),
        "col_blocks": set_ends(jax.random.randint(arg_keys[2], (N_GRP, N_AUX, KMAX), 0, NBG), jax.random.fold_in(arg_keys[2], 1), 0, NBG - 1).astype(jnp.int32),
        "aux_blocks": set_ends(jax.random.randint(arg_keys[3], (N_GRP, N_AUX, KMAX), 0, PDEV // PB), jax.random.fold_in(arg_keys[3], 1), 0, (PDEV // PB) - 1).astype(jnp.int32),
        "tile_counts": draw_tile_counts(jax.random.fold_in(arg_keys[7], 71), 0),
        "occ_coeffs": centred(arg_keys[5], (O, NAO), BLK ** -0.5, 0.5, ((1, 8),)),
        "vir_coeffs": centred(arg_keys[6], (NAO, V), BLK ** -0.5, 0.5, ((0, 8),)),
    }


def reference(integral_tiles, row_blocks, col_blocks, aux_blocks, tile_counts, occ_coeffs, vir_coeffs):
    flat_tiles = integral_tiles.reshape(N_GRP * N_AUX * KMAX, PB, BLK, BLK)
    flat_rows = row_blocks.reshape(-1)
    flat_cols = col_blocks.reshape(-1)
    flat_aux = aux_blocks.reshape(-1)
    result = jnp.zeros((O * V, NAUX), jnp.float32)

    def step(slot, result):
        group = slot // (N_AUX * KMAX)
        column = (slot // KMAX) % N_AUX
        inner = slot % KMAX
        tile = flat_tiles[slot].astype(jnp.float32)
        occ_block = lax.dynamic_slice_in_dim(occ_coeffs, (flat_rows[slot] * BLK).astype(jnp.int32), BLK, 1).astype(jnp.float32)
        half_tile = jnp.einsum('im,pmn->ipn', occ_block, tile).astype(jnp.bfloat16).astype(jnp.float32)
        vir_start = ((group * NBG + flat_cols[slot]) * BLK).astype(jnp.int32)
        vir_block = lax.dynamic_slice_in_dim(vir_coeffs, vir_start, BLK, 0).astype(jnp.float32)
        term = jnp.einsum('na,ipn->iap', vir_block, half_tile).reshape(O * V, PB)
        keep = (inner < tile_counts[group, column]).astype(jnp.float32)
        start = (column * PDEV + flat_aux[slot] * PB).astype(jnp.int32)
        current = lax.dynamic_slice_in_dim(result, start, PB, 1)
        return lax.dynamic_update_slice_in_dim(result, current + keep * term, start, 1)

    return lax.fori_loop(0, N_GRP * N_AUX * KMAX, step, result)
```

```python
import functools

import jax
import jax.numpy as jnp
from jax import lax
from jax.experimental import pallas as pl
from jax.experimental.pallas import tpu as pltpu
from jax.sharding import PartitionSpec as P

PDEV = 512


def half_kernel(rows_ref, count_ref, occ_ref, tile_ref, half_ref, stage_ref):
    slot = pl.program_id(0)
    orbitals, _, pb, blk = half_ref.shape

    @pl.when(slot < count_ref[0])
    def _():
        occ = occ_ref[...].astype(jnp.float32)[:orbitals]
        zero = jnp.zeros_like(occ)
        upper = jnp.concatenate([occ, zero], axis=1)
        lower = jnp.concatenate([zero, occ], axis=1)
        pair = jnp.concatenate([upper, lower], axis=0).astype(jnp.bfloat16)
        for p in range(0, pb, 2):
            rhs = tile_ref[0, p : p + 2].reshape(2 * blk, blk)
            stage_ref[p * orbitals : (p + 2) * orbitals, :] = jnp.dot(
                pair, rhs, preferred_element_type=jnp.float32
            )
        for i in range(orbitals):
            half_ref[i, 0] = stage_ref[pl.ds(i, pb, stride=orbitals), :].astype(jnp.bfloat16)

    @pl.when(slot >= count_ref[0])
    def _():
        half_ref[...] = jnp.zeros_like(half_ref)


def half_transform(tiles, rows, count, occ_ext, orbitals):
    kmax, pb, blk, _ = tiles.shape
    return pl.pallas_call(
        half_kernel,
        grid_spec=pltpu.PrefetchScalarGridSpec(
            num_scalar_prefetch=2,
            grid=(kmax,),
            in_specs=[
                pl.BlockSpec((occ_ext.shape[0], blk), lambda k, rows, count: (0, rows[k])),
                pl.BlockSpec(
                    (1, pb, blk, blk), lambda k, rows, count: (jnp.minimum(k, count[0] - 1), 0, 0, 0)
                ),
            ],
            out_specs=pl.BlockSpec((orbitals, 1, pb, blk), lambda k, rows, count: (0, k, 0, 0)),
            scratch_shapes=[pltpu.VMEM((pb * orbitals, blk), jnp.float32)],
        ),
        out_shape=jax.ShapeDtypeStruct((orbitals, kmax, pb, blk), jnp.bfloat16),
        compiler_params=pltpu.CompilerParams(vmem_limit_bytes=24 << 20),
        cost_estimate=pl.CostEstimate(
            flops=2 * tiles.size * orbitals * 2, bytes_accessed=tiles.size * 2, transcendentals=0
        ),
        name="half_transform",
    )(rows, count, occ_ext, tiles)


def pair_kernel(kmax, pb, code_ref, where_ref, half_ref, vir_ref, own_ref, send_ref, dense_ref, sum_ref, turn_ref):
    g = pl.program_id(0)
    per_dev = PDEV // pb
    blk = half_ref.shape[2]
    dense_ref[...] = jnp.zeros_like(dense_ref)
    codes = [code_ref[g * kmax + k] for k in range(kmax)]
    again = []
    for k in range(kmax):
        seen = jnp.bool_(False)
        for j in range(k):
            seen = jnp.logical_or(seen, codes[j] == codes[k])
        again.append(seen)
    places = []
    for k in range(kmax):
        at = codes[k] - 1
        col = pl.multiple_of(at // per_dev * blk, blk)
        row = pl.multiple_of(at % per_dev * pb, pb)
        places.append((row, col))

        @pl.when(jnp.logical_and(codes[k] > 0, jnp.logical_not(again[k])))
        def _():
            dense_ref[pl.ds(row, pb), pl.ds(col, blk)] = half_ref[0, k * pb : (k + 1) * pb, :]

    product = jnp.dot(dense_ref[...], vir_ref[...], preferred_element_type=jnp.float32)

    @pl.when(g == 0)
    def _():
        sum_ref[...] = product

    @pl.when(g > 0)
    def _():
        sum_ref[...] += product

    for k in range(kmax):
        row, col = places[k]

        @pl.when(jnp.logical_and(codes[k] > 0, again[k]))
        def _():
            sum_ref[pl.ds(row, pb), :] += jnp.dot(
                half_ref[0, k * pb : (k + 1) * pb, :],
                vir_ref[pl.ds(col, blk), :],
                preferred_element_type=jnp.float32,
            )

    @pl.when(g == pl.num_programs(0) - 1)
    def _():
        turn_ref[...] = sum_ref[...].T
        vb = own_ref.shape[0]
        mine = where_ref[0]
        own_ref[...] = turn_ref[pl.ds(pl.multiple_of(mine * vb, vb), vb), :]
        for j in range(send_ref.shape[0]):
            other = jnp.bitwise_xor(mine, j + 1)
            send_ref[j] = turn_ref[pl.ds(pl.multiple_of(other * vb, vb), vb), :].astype(jnp.bfloat16)


def pair_transform(halves, codes, vir, mine, kmax, pb, vb):
    group = halves.shape[0]
    blk = halves.shape[2]
    depth, width = vir.shape[0] // group, vir.shape[1]
    others = width // vb - 1
    return pl.pallas_call(
        functools.partial(pair_kernel, kmax, pb),
        grid_spec=pltpu.PrefetchScalarGridSpec(
            num_scalar_prefetch=2,
            grid=(group,),
            in_specs=[
                pl.BlockSpec((1, kmax * pb, blk), lambda g, *_: (g, 0, 0)),
                pl.BlockSpec((depth, width), lambda g, *_: (g, 0)),
            ],
            out_specs=[
                pl.BlockSpec((vb, PDEV), lambda g, *_: (0, 0)),
                pl.BlockSpec((others, vb, PDEV), lambda g, *_: (0, 0, 0)),
            ],
            scratch_shapes=[
                pltpu.VMEM((PDEV, depth), jnp.bfloat16),
                pltpu.VMEM((PDEV, width), jnp.float32),
                pltpu.VMEM((width, PDEV), jnp.float32),
            ],
        ),
        out_shape=[
            jax.ShapeDtypeStruct((vb, PDEV), jnp.float32),
            jax.ShapeDtypeStruct((others, vb, PDEV), jnp.bfloat16),
        ],
        compiler_params=pltpu.CompilerParams(vmem_limit_bytes=24 << 20),
        cost_estimate=pl.CostEstimate(
            flops=2 * PDEV * vir.size, bytes_accessed=vir.size * 2 + halves.size * 2, transcendentals=0
        ),
        name="pair_transform",
    )(codes, mine, halves, vir)


def place_kernel(where_ref, first_ref, second_ref, got_first_ref, got_second_ref, out_ref):
    group = pl.program_id(0)
    side = pl.program_id(1)

    @pl.when(jnp.logical_and(group == 0, side == 0))
    def _():
        out_ref[...] = first_ref[...]

    @pl.when(jnp.logical_and(group == 0, side == 1))
    def _():
        out_ref[...] = second_ref[...]

    @pl.when(jnp.logical_and(group > 0, side == 0))
    def _():
        out_ref[...] = got_first_ref[0].astype(jnp.float32)

    @pl.when(jnp.logical_and(group > 0, side == 1))
    def _():
        out_ref[...] = got_second_ref[0].astype(jnp.float32)


def place(where, first, second, got_first, got_second, aux_size):
    vb = first.shape[0]
    half = pl.BlockSpec((vb, PDEV), lambda j, s, where: (0, 0))
    got = pl.BlockSpec((1, vb, PDEV), lambda j, s, where: (jnp.maximum(j - 1, 0), 0, 0))

    def column(j, s, where):
        return 0, jnp.bitwise_xor(where[0], j) * 2 + jnp.bitwise_xor(where[1], s)

    return pl.pallas_call(
        place_kernel,
        grid_spec=pltpu.PrefetchScalarGridSpec(
            num_scalar_prefetch=1,
            grid=(aux_size // 2, 2),
            in_specs=[half, half, got, got],
            out_specs=pl.BlockSpec((vb, PDEV), column),
        ),
        out_shape=jax.ShapeDtypeStruct((vb, aux_size * PDEV), jnp.float32),
        cost_estimate=pl.CostEstimate(
            flops=0, bytes_accessed=vb * aux_size * PDEV * 8, transcendentals=0
        ),
        name="place",
    )(where, first, second, got_first, got_second)


def shards(integral_tiles, row_blocks, col_blocks, aux_blocks, tile_counts, occ_coeffs, vir_coeffs):
    group_size = lax.axis_size("grp")
    aux_size = lax.axis_size("aux")
    aux = lax.axis_index("aux")
    kmax, pb, blk = integral_tiles.shape[2:5]
    orbitals, own_ao = occ_coeffs.shape
    virtuals = vir_coeffs.shape[1]
    vb = virtuals * orbitals // (group_size * aux_size)
    count = tile_counts[0, 0]

    def swap(x, step):
        return lax.ppermute(x, "aux", [(a, a ^ step) for a in range(aux_size)])

    code = col_blocks[0, 0] * (PDEV // pb) + aux_blocks[0, 0] + 1
    code = jnp.where(jnp.arange(kmax) < count, code, 0).astype(jnp.bfloat16)
    extra = jnp.zeros((8, own_ao), jnp.bfloat16).at[0, :kmax].set(code)
    occ_ext = lax.all_gather(
        jnp.concatenate([occ_coeffs, extra], axis=0), "grp", axis=1, tiled=True
    )
    codes = occ_ext[orbitals].reshape(group_size, own_ao)[:, :kmax].astype(jnp.int32).reshape(-1)
    other_codes = swap(codes, 1)

    parity = vir_coeffs.reshape(own_ao, aux_size // 2, 2, vb)
    parity = lax.dynamic_index_in_dim(parity, aux % 2, 2, keepdims=False).reshape(own_ao, -1)
    vir = lax.all_gather(parity, "grp", axis=0, tiled=True)

    halves = half_transform(
        integral_tiles[0, 0], row_blocks[0, 0], tile_counts[0], occ_ext, orbitals
    ).reshape(orbitals, kmax * pb, blk)
    halves = lax.all_to_all(halves, "grp", split_axis=0, concat_axis=0, tiled=True)
    other_halves = swap(halves, 1)

    where = jnp.stack([aux // 2, aux % 2]).astype(jnp.int32)
    first, send_first = pair_transform(halves, codes, vir, where, kmax, pb, vb)
    second, send_second = pair_transform(other_halves, other_codes, vir, where, kmax, pb, vb)

    def trade(send):
        return jnp.stack([swap(send[j - 1], 2 * j) for j in range(1, aux_size // 2)])

    return place(where, first, second, trade(send_first), trade(send_second), aux_size)


def solution(mesh):
    in_specs = (
        P("grp", "aux", None, None, None, None),
        P("grp", "aux", None),
        P("grp", "aux", None),
        P("grp", "aux", None),
        P("grp", "aux"),
        P(None, "grp"),
        P("grp", None),
    )
    out_specs = P(("grp", "aux"), None)
    return jax.shard_map(shards, mesh=mesh, in_specs=in_specs, out_specs=out_specs, check_vma=False)
```

```python
import functools

import jax
import jax.numpy as jnp
from jax import lax
from jax.experimental import pallas as pl
from jax.experimental.pallas import tpu as pltpu
from jax.sharding import PartitionSpec as P

PDEV = 512
META = 16
FIELD = 16


def whole(shape):
    return pl.BlockSpec(shape, lambda n, *_: (0,) * len(shape))


def half_kernel(index_ref, occ_ref, tiles_hbm, half_ref, tile_ref, stage_ref, sems):
    kmax, pb, blk, _ = tile_ref.shape
    rows_ref, cols_ref, aux_ref = (index_ref.at[pl.ds(n * kmax, kmax)] for n in range(3))
    orbitals = half_ref.shape[0]
    ao_blocks = occ_ref.shape[2] // blk
    count = index_ref[3 * kmax]

    def fetch(k):
        return pltpu.make_async_copy(tiles_hbm.at[k], tile_ref.at[k], sems.at[k])

    for k in range(kmax):

        @pl.when(k < count)
        def _():
            fetch(k).start()

    lanes = lax.broadcasted_iota(jnp.int32, (META, blk), 1)
    meta = jnp.zeros((META, blk), jnp.int32)
    for k in range(kmax):
        again = jnp.bool_(False)
        for j in range(k):
            same = jnp.logical_and(cols_ref[j] == cols_ref[k], aux_ref[j] == aux_ref[k])
            again = jnp.logical_or(again, same)
        again = jnp.logical_and(again, k < count)
        row = aux_ref[k] * pb
        first = jnp.where(jnp.logical_or(again, k >= count), PDEV, row)
        for n, value in enumerate((first, cols_ref[k] * blk, again.astype(jnp.int32), row)):
            meta = jnp.where(lanes == n * FIELD + k, value, meta)
    meta = meta.astype(jnp.float32).astype(jnp.bfloat16)
    for i in range(orbitals):
        half_ref[i, kmax * pb :, :] = meta

    for k in range(kmax):

        @pl.when(k < count)
        def _():
            row = rows_ref[k]
            lane = pl.multiple_of(row % ao_blocks * blk, blk)
            occ = occ_ref[row // ao_blocks, :, pl.ds(lane, blk)].astype(jnp.float32)
            zero = jnp.zeros_like(occ)
            upper = jnp.concatenate([occ, zero], axis=1)
            lower = jnp.concatenate([zero, occ], axis=1)
            pair = jnp.concatenate([upper, lower], axis=0).astype(jnp.bfloat16)
            stage = stage_ref.at[k % 2]
            fetch(k).wait()
            for p in range(0, pb, 2):
                rhs = tile_ref[k, p : p + 2].reshape(2 * blk, blk)
                stage[p * orbitals : (p + 2) * orbitals, :] = jnp.dot(
                    pair, rhs, preferred_element_type=jnp.float32
                )
            for i in range(orbitals):
                half_ref[i, k * pb : (k + 1) * pb, :] = stage[
                    pl.ds(i, pb, stride=orbitals), :
                ].astype(jnp.bfloat16)

        @pl.when(k >= count)
        def _():
            half_ref[:, k * pb : (k + 1) * pb, :] = jnp.zeros((orbitals, pb, blk), jnp.bfloat16)


def half_transform(tiles, index, occ):
    kmax, pb, blk, _ = tiles.shape
    orbitals = occ.shape[1]
    out = (orbitals, kmax * pb + META, blk)
    return pl.pallas_call(
        half_kernel,
        grid_spec=pltpu.PrefetchScalarGridSpec(
            num_scalar_prefetch=1,
            grid=(1,),
            in_specs=[whole(occ.shape), pl.BlockSpec(memory_space=pl.ANY)],
            out_specs=whole(out),
            scratch_shapes=[
                pltpu.VMEM(tiles.shape, jnp.bfloat16),
                pltpu.VMEM((2, pb * orbitals, blk), jnp.float32),
                pltpu.SemaphoreType.DMA((kmax,)),
            ],
        ),
        out_shape=jax.ShapeDtypeStruct(out, jnp.bfloat16),
        compiler_params=pltpu.CompilerParams(vmem_limit_bytes=56 << 20),
        cost_estimate=pl.CostEstimate(
            flops=4 * tiles.size * orbitals, bytes_accessed=tiles.size * 2, transcendentals=0
        ),
        name="half_transform",
    )(index, occ, tiles)


def pair_kernel(kmax, pb, group, where_ref, half_ref, *refs):
    vir_refs, refs = refs[:group], refs[group:]
    own_ref, send_ref, dense_ref, sum_ref, turn_ref, meta_ref, code_ref, again_ref, sem = refs
    depth = vir_refs[0].shape[0]
    blk = half_ref.shape[2]
    for g in range(group):
        meta_ref[g : g + 1, :] = half_ref[g, kmax * pb :, :].astype(jnp.float32)[:1].astype(jnp.int32)
    copy = pltpu.make_async_copy(meta_ref, code_ref, sem)
    copy.start()
    dense_ref[:PDEV, :] = jnp.zeros((PDEV, group * depth), jnp.bfloat16)
    copy.wait()

    def scatter(step, repeats):
        g = where_ref[2 + step]
        for k in range(kmax):
            row = pl.multiple_of(code_ref[g, k], pb)
            lane = pl.multiple_of(step * depth + code_ref[g, FIELD + k], blk)
            dense_ref[pl.ds(row, pb), pl.ds(lane, blk)] = half_ref[g, k * pb : (k + 1) * pb, :]
            again_ref[repeats] = step * kmax + k
            repeats = repeats + code_ref[g, 2 * FIELD + k]
        return repeats

    repeats = lax.fori_loop(0, group, scatter, jnp.int32(0))
    vir = jnp.concatenate([ref[...] for ref in vir_refs], axis=0)
    sum_ref[...] = jnp.dot(dense_ref[:PDEV, :], vir, preferred_element_type=jnp.float32)

    def repeat(n, carry):
        slot = again_ref[n]
        step, k = slot // kmax, slot % kmax
        g = where_ref[2 + step]
        row = pl.multiple_of(code_ref[g, 3 * FIELD + k], pb)
        lane = pl.multiple_of(code_ref[g, FIELD + k], blk)
        tile = half_ref[g, pl.ds(pl.multiple_of(k * pb, pb), pb), :]
        for d in range(group):

            @pl.when(step == d)
            def _():
                sum_ref[pl.ds(row, pb), :] += jnp.dot(
                    tile, vir_refs[d][pl.ds(lane, blk), :], preferred_element_type=jnp.float32
                )

        return carry

    lax.fori_loop(0, repeats, repeat, 0)
    turn_ref[...] = sum_ref[...].T
    vb = own_ref.shape[0]
    mine = where_ref[0]
    own_ref[...] = turn_ref[pl.ds(pl.multiple_of(mine * vb, vb), vb), :]
    for j in range(send_ref.shape[0]):
        other = jnp.bitwise_xor(mine, j + 1)
        send_ref[j] = turn_ref[pl.ds(pl.multiple_of(other * vb, vb), vb), :].astype(jnp.bfloat16)


def pair_transform(halves, virs, where, kmax, pb, vb):
    group, _, blk = halves.shape
    depth, width = virs[0].shape
    others = width // vb - 1
    return pl.pallas_call(
        functools.partial(pair_kernel, kmax, pb, group),
        grid_spec=pltpu.PrefetchScalarGridSpec(
            num_scalar_prefetch=1,
            grid=(1,),
            in_specs=[whole(halves.shape)] + [whole((depth, width))] * group,
            out_specs=[whole((vb, PDEV)), whole((others, vb, PDEV))],
            scratch_shapes=[
                pltpu.VMEM((PDEV + pb, group * depth), jnp.bfloat16),
                pltpu.VMEM((PDEV, width), jnp.float32),
                pltpu.VMEM((width, PDEV), jnp.float32),
                pltpu.VMEM((group, blk), jnp.int32),
                pltpu.SMEM((group, blk), jnp.int32),
                pltpu.SMEM((group * kmax + 1,), jnp.int32),
                pltpu.SemaphoreType.DMA,
            ],
        ),
        out_shape=[
            jax.ShapeDtypeStruct((vb, PDEV), jnp.float32),
            jax.ShapeDtypeStruct((others, vb, PDEV), jnp.bfloat16),
        ],
        compiler_params=pltpu.CompilerParams(vmem_limit_bytes=28 << 20),
        cost_estimate=pl.CostEstimate(
            flops=4 * PDEV * group * depth * width,
            bytes_accessed=group * depth * width * 2 + halves.size * 2,
            transcendentals=0,
        ),
        name="pair_transform",
    )(where, halves, *virs)


def place_kernel(where_ref, first_ref, second_ref, got_first_ref, got_second_ref, out_hbm, wide_ref, sems):
    pairs = out_hbm.shape[1] // (2 * PDEV)
    copies = []
    for j in range(pairs):
        for s in range(2):
            if j == 0:
                src = (first_ref, second_ref)[s]
            else:
                n = 2 * (j - 1) + s
                wide_ref[n] = (got_first_ref, got_second_ref)[s][j - 1].astype(jnp.float32)
                src = wide_ref.at[n]
            block = jnp.bitwise_xor(where_ref[0], j) * 2 + jnp.bitwise_xor(where_ref[1], s)
            lane = pl.multiple_of(block * PDEV, PDEV)
            copies.append(
                pltpu.make_async_copy(src, out_hbm.at[:, pl.ds(lane, PDEV)], sems.at[2 * j + s])
            )
            copies[-1].start()
    for copy in copies:
        copy.wait()


def place(where, first, second, got_first, got_second, aux_size):
    vb = first.shape[0]
    return pl.pallas_call(
        place_kernel,
        grid_spec=pltpu.PrefetchScalarGridSpec(
            num_scalar_prefetch=1,
            grid=(1,),
            in_specs=[whole(x.shape) for x in (first, second, got_first, got_second)],
            out_specs=pl.BlockSpec(memory_space=pl.ANY),
            scratch_shapes=[
                pltpu.VMEM((aux_size - 2, vb, PDEV), jnp.float32),
                pltpu.SemaphoreType.DMA((aux_size,)),
            ],
        ),
        out_shape=jax.ShapeDtypeStruct((vb, aux_size * PDEV), jnp.float32),
        cost_estimate=pl.CostEstimate(
            flops=0, bytes_accessed=vb * aux_size * PDEV * 8, transcendentals=0
        ),
        name="place",
    )(where, first, second, got_first, got_second)


def copy_kernel(where_ref, in_ref, out_ref):
    out_ref[...] = in_ref[...]


def vir_columns(vir, aux, aux_size, vb):
    rows = vir.shape[0]
    if vb % 128:
        chosen = vir.reshape(rows, aux_size // 2, 2, vb)
        return lax.dynamic_index_in_dim(chosen, aux % 2, 2, keepdims=False).reshape(rows, -1)
    return pl.pallas_call(
        copy_kernel,
        grid_spec=pltpu.PrefetchScalarGridSpec(
            num_scalar_prefetch=1,
            grid=(aux_size // 2,),
            in_specs=[pl.BlockSpec((rows, vb), lambda j, where: (0, 2 * j + where[0]))],
            out_specs=pl.BlockSpec((rows, vb), lambda j, where: (0, j)),
        ),
        out_shape=jax.ShapeDtypeStruct((rows, aux_size // 2 * vb), vir.dtype),
        name="vir_columns",
    )((aux % 2).astype(jnp.int32)[None], vir)


def shards(integral_tiles, row_blocks, col_blocks, aux_blocks, tile_counts, occ_coeffs, vir_coeffs):
    group_size = lax.axis_size("grp")
    aux_size = lax.axis_size("aux")
    aux = lax.axis_index("aux")
    kmax, pb = integral_tiles.shape[2:4]
    orbitals = occ_coeffs.shape[0]
    virtuals = vir_coeffs.shape[1]
    vb = virtuals * orbitals // (group_size * aux_size)

    def swap(x, step):
        return lax.ppermute(x, "aux", [(a, a ^ step) for a in range(aux_size)])

    def hop(x, steps):
        return lax.ppermute(x, "grp", [(g, g ^ steps[g % 2]) for g in range(group_size)])

    occ = jnp.broadcast_to(occ_coeffs[None], (group_size, *occ_coeffs.shape))
    occ = lax.all_to_all(occ, "grp", split_axis=0, concat_axis=0, tiled=True)

    core = lax.axis_index("grp") % 2
    own = vir_columns(vir_coeffs, aux, aux_size, vb)
    near = hop(own, (2, 4))
    far = hop(own, (4, 2))
    occ, near, far = lax.optimization_barrier((occ, near, far))
    across = hop(near, (4, 2))
    virs = [own, near, far, across]
    virs = virs + [hop(vir, (1, 1)) for vir in virs]

    index = [x[0, 0] for x in (row_blocks, col_blocks, aux_blocks)] + [tile_counts[0]]
    halves = half_transform(integral_tiles[0, 0], jnp.concatenate(index), occ)
    halves = lax.all_to_all(halves, "grp", split_axis=0, concat_axis=0, tiled=True)
    other_halves = swap(halves, 1)

    moved = [0, 2 + 2 * core, 4 - 2 * core, 6, 1, 5 - 2 * core, 3 + 2 * core, 7]
    moved = [jnp.bitwise_xor(lax.axis_index("grp"), step) for step in moved]
    where = jnp.stack([aux // 2, aux % 2] + moved).astype(jnp.int32)
    first, send_first = pair_transform(halves, virs, where, kmax, pb, vb)
    other_halves, _ = lax.optimization_barrier((other_halves, send_first))
    second, send_second = pair_transform(other_halves, virs, where, kmax, pb, vb)

    def trade(send):
        if aux_size == 4:
            return swap(send, 2)
        return jnp.stack([swap(send[j - 1], 2 * j) for j in range(1, aux_size // 2)])

    return place(where, first, second, trade(send_first), trade(send_second), aux_size)


def solution(mesh):
    in_specs = (
        P("grp", "aux", None, None, None, None),
        P("grp", "aux", None),
        P("grp", "aux", None),
        P("grp", "aux", None),
        P("grp", "aux"),
        P(None, "grp"),
        P("grp", None),
    )
    out_specs = P(("grp", "aux"), None)
    return jax.shard_map(shards, mesh=mesh, in_specs=in_specs, out_specs=out_specs, check_vma=False)
```

```python
import functools

import jax
import jax.numpy as jnp
from jax import lax
from jax.experimental import pallas as pl
from jax.experimental.pallas import tpu as pltpu
from jax.sharding import PartitionSpec as P

PDEV = 512
META = 16
PAIR_LIMIT = 40
PLACE_LIMIT = 40
FIELD = 16


def whole(shape):
    return pl.BlockSpec(shape, lambda n, *_: (0,) * len(shape))


def row_of(k, kmax, pb):
    return k * pb + (META if k >= kmax // 2 else 0)


def half_kernel(index_ref, occ_ref, tiles_hbm, half_ref, tile_ref, stage_ref, sems):
    kmax, pb, blk, _ = tile_ref.shape
    rows_ref, cols_ref, aux_ref = (index_ref.at[pl.ds(n * kmax, kmax)] for n in range(3))
    orbitals = half_ref.shape[0]
    ao_blocks = occ_ref.shape[2] // blk
    count = index_ref[3 * kmax]

    def fetch(k):
        return pltpu.make_async_copy(tiles_hbm.at[k], tile_ref.at[k], sems.at[k])

    for k in range(kmax):

        @pl.when(k < count)
        def _():
            fetch(k).start()

    lanes = lax.broadcasted_iota(jnp.int32, (META, blk), 1)
    meta = jnp.zeros((META, blk), jnp.int32)
    for k in range(kmax):
        again = jnp.bool_(False)
        for j in range(k):
            same = jnp.logical_and(cols_ref[j] == cols_ref[k], aux_ref[j] == aux_ref[k])
            again = jnp.logical_or(again, same)
        again = jnp.logical_and(again, k < count)
        row = aux_ref[k] * pb
        first = jnp.where(jnp.logical_or(again, k >= count), PDEV, row)
        for n, value in enumerate((first, cols_ref[k] * blk, again.astype(jnp.int32), row)):
            meta = jnp.where(lanes == n * FIELD + k, value, meta)
    meta = meta.astype(jnp.float32).astype(jnp.bfloat16)
    split = kmax // 2 * pb
    for i in range(orbitals):
        half_ref[i, split : split + META, :] = meta

    for k in range(kmax):
        at = row_of(k, kmax, pb)

        @pl.when(k < count)
        def _(k=k, at=at):
            row = rows_ref[k]
            lane = pl.multiple_of(row % ao_blocks * blk, blk)
            occ = occ_ref[row // ao_blocks, :, pl.ds(lane, blk)].astype(jnp.float32)
            zero = jnp.zeros_like(occ)
            upper = jnp.concatenate([occ, zero], axis=1)
            lower = jnp.concatenate([zero, occ], axis=1)
            pair = jnp.concatenate([upper, lower], axis=0).astype(jnp.bfloat16)
            stage = stage_ref.at[k % 2]
            fetch(k).wait()
            for p in range(0, pb, 2):
                rhs = tile_ref[k, p : p + 2].reshape(2 * blk, blk)
                stage[p * orbitals : (p + 2) * orbitals, :] = jnp.dot(
                    pair, rhs, preferred_element_type=jnp.float32
                )
            for i in range(orbitals):
                part = stage[pl.ds(i, pb, stride=orbitals), :].astype(jnp.bfloat16)
                half_ref[i, at : at + pb, :] = part

        @pl.when(k >= count)
        def _(at=at):
            empty = jnp.zeros((orbitals, pb, blk), jnp.bfloat16)
            half_ref[:, at : at + pb, :] = empty


def half_transform(tiles, index, occ):
    kmax, pb, blk, _ = tiles.shape
    orbitals = occ.shape[1]
    out = (orbitals, kmax * pb + META, blk)
    return pl.pallas_call(
        half_kernel,
        grid_spec=pltpu.PrefetchScalarGridSpec(
            num_scalar_prefetch=1,
            grid=(1,),
            in_specs=[whole(occ.shape), pl.BlockSpec(memory_space=pl.ANY)],
            out_specs=whole(out),
            scratch_shapes=[
                pltpu.VMEM(tiles.shape, jnp.bfloat16),
                pltpu.VMEM((2, pb * orbitals, blk), jnp.float32),
                pltpu.SemaphoreType.DMA((kmax,)),
            ],
        ),
        out_shape=jax.ShapeDtypeStruct(out, jnp.bfloat16),
        compiler_params=pltpu.CompilerParams(vmem_limit_bytes=52 << 20),
        cost_estimate=pl.CostEstimate(
            flops=4 * tiles.size * orbitals, bytes_accessed=tiles.size * 2, transcendentals=0
        ),
        name="half_transform",
    )(index, occ, tiles)


def pair_kernel(kmax, pb, group, vb, kind, inputs, side, where_ref, *refs):
    half_refs, refs = refs[:inputs], refs[inputs:]
    vir_hbm, refs = refs[:group], refs[group:]
    vir_ref, dense_ref, sum_ref, turn_ref, meta_ref, code_ref, again_ref, sem, sems = refs[-9:]
    results = refs[-9 - (2 if kind == "both" else 1) : -9]
    depth = vir_hbm[0].shape[0]
    blk = meta_ref.shape[1]
    low, high = columns_for(kind, vir_ref.shape[1] if kind == "both" else vir_hbm[0].shape[1], vb)
    fetches = [
        pltpu.make_async_copy(
            vir_hbm[d].at[:, pl.ds(low, high - low)], vir_ref.at[pl.ds(d * depth, depth), :], sems.at[d]
        )
        for d in range(group)
    ]
    for fetch in fetches:
        fetch.start()
    split = kmax // 2 * pb
    for g in range(group):
        meta_ref[g : g + 1, :] = (
            half_refs[0][g, split : split + META, :].astype(jnp.float32)[:1].astype(jnp.int32)
        )
    copy = pltpu.make_async_copy(meta_ref, code_ref, sem)
    copy.start()
    dense_ref[:PDEV, :] = jnp.zeros((PDEV, group * depth), jnp.bfloat16)
    copy.wait()

    def source(k):
        at = row_of(k, kmax, pb)
        if inputs == 2 and k >= kmax // 2:
            return half_refs[1], at - split - META
        return half_refs[0], at

    def scatter(step, repeats):
        g = where_ref[2 + step]
        for k in range(kmax):
            ref, at = source(k)
            row = pl.multiple_of(code_ref[g, k], pb)
            lane = pl.multiple_of(step * depth + code_ref[g, FIELD + k], blk)
            dense_ref[pl.ds(row, pb), pl.ds(lane, blk)] = ref[g, at : at + pb, :]
            again_ref[repeats] = step * kmax + k
            repeats = repeats + code_ref[g, 2 * FIELD + k]
        return repeats

    repeats = lax.fori_loop(0, group, scatter, jnp.int32(0))
    for fetch in fetches:
        fetch.wait()
    sum_ref[...] = jnp.dot(dense_ref[:PDEV, :], vir_ref[...], preferred_element_type=jnp.float32)

    def repeat(n, carry):
        slot = again_ref[n]
        step, k = slot // kmax, slot % kmax
        g = where_ref[2 + step]
        row = pl.multiple_of(code_ref[g, 3 * FIELD + k], pb)
        lane = pl.multiple_of(step * depth + code_ref[g, FIELD + k], blk)

        def add(ref, at):
            sum_ref[pl.ds(row, pb), :] += jnp.dot(
                ref[g, pl.ds(pl.multiple_of(at, META), pb), :],
                vir_ref[pl.ds(lane, blk), :],
                preferred_element_type=jnp.float32,
            )

        late = k >= kmax // 2

        @pl.when(late)
        def _():
            if inputs == 2:
                add(half_refs[1], k * pb - split)
            else:
                add(half_refs[0], k * pb + META)

        @pl.when(jnp.logical_not(late))
        def _():
            add(half_refs[0], k * pb)

        return carry

    lax.fori_loop(0, repeats, repeat, 0)
    turn_ref[...] = sum_ref[...].T
    offset = 0
    if kind != "send":
        offset = vb
        column = pl.multiple_of(where_ref[side] * PDEV, PDEV)
        copy = pltpu.make_async_copy(
            turn_ref.at[:vb], results[-1].at[:, pl.ds(column, PDEV)], sems.at[group]
        )
        copy.start()
    if kind != "own":
        for j in range(results[0].shape[0]):
            results[0][j] = turn_ref[offset + j * vb : offset + (j + 1) * vb].astype(jnp.bfloat16)
    if kind != "send":
        copy.wait()


def columns_for(kind, width, vb):
    return {"both": (0, width), "own": (0, vb), "send": (vb, width)}[kind]


def pair_transform(kind, halves, virs, where, kmax, pb, vb, columns=0, result=None):
    group, _, blk = halves[0].shape
    depth, width = virs[0].shape
    others = width // vb - 1
    low, high = columns_for(kind, width, vb)
    anywhere = pl.BlockSpec(memory_space=pl.ANY)
    out_specs, out_shape = [], []
    if kind != "own":
        out_specs.append(whole((others, vb, PDEV)))
        out_shape.append(jax.ShapeDtypeStruct((others, vb, PDEV), jnp.bfloat16))
    if kind != "send":
        out_specs.append(anywhere)
        out_shape.append(jax.ShapeDtypeStruct((vb, columns), jnp.float32))
    return pl.pallas_call(
        functools.partial(pair_kernel, kmax, pb, group, vb, kind, len(halves), int(result is not None)),
        grid_spec=pltpu.PrefetchScalarGridSpec(
            num_scalar_prefetch=1,
            grid=(1,),
            in_specs=[whole(x.shape) for x in halves] + [anywhere] * (group + (result is not None)),
            out_specs=out_specs,
            scratch_shapes=[
                pltpu.VMEM((group * depth, high - low), jnp.bfloat16),
                pltpu.VMEM((PDEV + pb, group * depth), jnp.bfloat16),
                pltpu.VMEM((PDEV, high - low), jnp.float32),
                pltpu.VMEM((high - low, PDEV), jnp.float32),
                pltpu.VMEM((group, blk), jnp.int32),
                pltpu.SMEM((group, blk), jnp.int32),
                pltpu.SMEM((group * kmax + 1,), jnp.int32),
                pltpu.SemaphoreType.DMA,
                pltpu.SemaphoreType.DMA((group + 1,)),
            ],
        ),
        out_shape=out_shape,
        input_output_aliases={} if result is None else {1 + len(halves) + group: 0},
        compiler_params=pltpu.CompilerParams(vmem_limit_bytes=PAIR_LIMIT << 20),
        cost_estimate=pl.CostEstimate(
            flops=4 * PDEV * group * depth * (high - low),
            bytes_accessed=group * depth * (high - low) * 2 + halves[0].size * 2,
            transcendentals=0,
        ),
        name=kind + "_part",
    )(where, *halves, *virs, *([] if result is None else [result]))


def place_kernel(side, where_ref, got_ref, _, out_hbm, wide_ref, sems):
    copies = []
    for j in range(got_ref.shape[0]):
        wide_ref[j] = got_ref[j].astype(jnp.float32)
        block = jnp.bitwise_xor(where_ref[side], 2 * (j + 1))
        lane = pl.multiple_of(block * PDEV, PDEV)
        copies.append(pltpu.make_async_copy(wide_ref.at[j], out_hbm.at[:, pl.ds(lane, PDEV)], sems.at[j]))
        copies[-1].start()
    for copy in copies:
        copy.wait()


def place(where, got, result, side):
    return pl.pallas_call(
        functools.partial(place_kernel, side),
        grid_spec=pltpu.PrefetchScalarGridSpec(
            num_scalar_prefetch=1,
            grid=(1,),
            in_specs=[whole(got.shape), pl.BlockSpec(memory_space=pl.ANY)],
            out_specs=pl.BlockSpec(memory_space=pl.ANY),
            scratch_shapes=[
                pltpu.VMEM(got.shape, jnp.float32),
                pltpu.SemaphoreType.DMA((got.shape[0],)),
            ],
        ),
        out_shape=jax.ShapeDtypeStruct(result.shape, jnp.float32),
        input_output_aliases={2: 0},
        cost_estimate=pl.CostEstimate(flops=0, bytes_accessed=got.size * 6, transcendentals=0),
        compiler_params=pltpu.CompilerParams(vmem_limit_bytes=PLACE_LIMIT << 20),
        name="place",
    )(where, got, result)


def open_kernel(vb, vir_hbm, occ_ref, occ_out_ref, out_ref, sems):
    aux = lax.axis_index("aux")
    copies = []
    for j in range(out_ref.shape[1] // vb):
        block = jnp.bitwise_xor(aux // 2, j) * 2 + aux % 2
        copies.append(
            pltpu.make_async_copy(
                vir_hbm.at[:, pl.ds(pl.multiple_of(block * vb, vb), vb)],
                out_ref.at[:, pl.ds(j * vb, vb)],
                sems.at[j],
            )
        )
        copies[-1].start()
    occ_out_ref[...] = jnp.broadcast_to(occ_ref[...][None], occ_out_ref.shape)
    for copy in copies:
        copy.wait()


def opening(vir, occ, group_size, aux, aux_size, vb):
    rows = vir.shape[0]
    parts = aux_size // 2
    copies = (group_size, *occ.shape)
    if vb % 128:
        order = jnp.bitwise_xor(aux // 2, jnp.arange(parts)) * 2 + aux % 2
        chosen = jnp.take(vir.reshape(rows, aux_size, vb), order, axis=1)
        return jnp.broadcast_to(occ[None], copies), chosen.reshape(rows, -1)
    vmem = pl.BlockSpec(memory_space=pltpu.VMEM)
    return pl.pallas_call(
        functools.partial(open_kernel, vb),
        in_specs=[pl.BlockSpec(memory_space=pl.ANY), vmem],
        out_specs=[vmem, vmem],
        scratch_shapes=[pltpu.SemaphoreType.DMA((parts,))],
        out_shape=[
            jax.ShapeDtypeStruct(copies, occ.dtype),
            jax.ShapeDtypeStruct((rows, parts * vb), vir.dtype),
        ],
        compiler_params=pltpu.CompilerParams(vmem_limit_bytes=60 << 20),
        name="opening",
    )(vir, occ)


def shards(integral_tiles, row_blocks, col_blocks, aux_blocks, tile_counts, occ_coeffs, vir_coeffs):
    group_size = lax.axis_size("grp")
    aux_size = lax.axis_size("aux")
    aux = lax.axis_index("aux")
    kmax, pb = integral_tiles.shape[2:4]
    orbitals = occ_coeffs.shape[0]
    virtuals = vir_coeffs.shape[1]
    vb = virtuals * orbitals // (group_size * aux_size)

    def swap(x, step):
        return lax.ppermute(x, "aux", [(a, a ^ step) for a in range(aux_size)])

    def hop(x, steps):
        return lax.ppermute(x, "grp", [(g, g ^ steps[g % 2]) for g in range(group_size)])

    occ, own = opening(vir_coeffs, occ_coeffs, group_size, aux, aux_size, vb)
    occ = lax.all_to_all(occ, "grp", split_axis=0, concat_axis=0, tiled=True)

    core = lax.axis_index("grp") % 2
    near = hop(own, (2, 4))
    far = hop(own, (4, 2))
    occ, near, far = lax.optimization_barrier((occ, near, far))
    across = hop(near, (4, 2))
    virs = [own, near, far, across]
    virs = virs + [hop(vir, (1, 1)) for vir in virs]

    index = [x[0, 0] for x in (row_blocks, col_blocks, aux_blocks)] + [tile_counts[0]]
    halves = half_transform(integral_tiles[0, 0], jnp.concatenate(index), occ)
    others = swap(halves, 1)
    halves = lax.all_to_all(halves, "grp", split_axis=0, concat_axis=0, tiled=True)
    others, halves = lax.optimization_barrier((others, halves))
    others = lax.all_to_all(others, "grp", split_axis=0, concat_axis=0, tiled=True)

    moved = [0, 2 + 2 * core, 4 - 2 * core, 6, 1, 5 - 2 * core, 3 + 2 * core, 7]
    moved = [jnp.bitwise_xor(lax.axis_index("grp"), step) for step in moved]
    where = jnp.stack([aux, jnp.bitwise_xor(aux, 1)] + moved).astype(jnp.int32)

    def trade(send):
        if aux_size == 4:
            return swap(send, 2)
        return jnp.stack([swap(send[j - 1], 2 * j) for j in range(1, aux_size // 2)])

    sizes = (kmax, pb, vb)
    columns = aux_size * PDEV
    if vb % 128:
        send_first, result = pair_transform("both", [halves], virs, where, *sizes, columns=columns)
        send_second, own_second = pair_transform("both", [others], virs, where, *sizes, columns=columns)
        got_first = trade(send_first)
        block = (jnp.bitwise_xor(aux, 1) * PDEV).astype(jnp.int32)
        own_second = lax.dynamic_slice_in_dim(own_second, (aux * PDEV).astype(jnp.int32), PDEV, 1)
        result = lax.dynamic_update_slice_in_dim(result, own_second, block, 1)
    else:
        (send_first,) = pair_transform("send", [halves], virs, where, *sizes)
        got_first = trade(send_first)
        others, _ = lax.optimization_barrier((others, send_first))
        (send_second,) = pair_transform("send", [others], virs, where, *sizes)
        others, halves, _ = lax.optimization_barrier((others, halves, send_second))
        (result,) = pair_transform("own", [halves], virs, where, *sizes, columns=columns)
        (result,) = pair_transform("own", [others], virs, where, *sizes, columns=columns, result=result)
    result = place(where, got_first, result, 0)
    return place(where, trade(send_second), result, 1)


def solution(mesh):
    in_specs = (
        P("grp", "aux", None, None, None, None),
        P("grp", "aux", None),
        P("grp", "aux", None),
        P("grp", "aux", None),
        P("grp", "aux"),
        P(None, "grp"),
        P("grp", None),
    )
    out_specs = P(("grp", "aux"), None)
    return jax.shard_map(shards, mesh=mesh, in_specs=in_specs, out_specs=out_specs, check_vma=False)
```

```python
import functools

import jax
import jax.numpy as jnp
from jax import lax
from jax.experimental import pallas as pl
from jax.experimental.pallas import tpu as pltpu
from jax.sharding import PartitionSpec as P

PDEV = 512
META = 16
PAIR_LIMIT = 40
PLACE_LIMIT = 40
FIELD = 16


def whole(shape):
    return pl.BlockSpec(shape, lambda n, *_: (0,) * len(shape))


def row_of(k, kmax, pb):
    return k * pb + (META if k >= kmax // 2 else 0)


def half_kernel(rows_ref, cols_ref, aux_ref, count_ref, occ_ref, tiles_hbm, half_ref, tile_ref, stage_ref, sems):
    kmax, pb, blk, _ = tile_ref.shape
    orbitals = half_ref.shape[0]
    ao_blocks = occ_ref.shape[2] // blk
    count = count_ref[0]

    def fetch(k):
        return pltpu.make_async_copy(tiles_hbm.at[k], tile_ref.at[k], sems.at[k])

    for k in range(kmax):

        @pl.when(k < count)
        def _():
            fetch(k).start()

    targets = []
    for k in range(kmax):
        target = jnp.int32(k)
        for j in reversed(range(k)):
            same = jnp.logical_and(cols_ref[j] == cols_ref[k], aux_ref[j] == aux_ref[k])
            target = jnp.where(same, j, target)
        targets.append(target)
    lanes = lax.broadcasted_iota(jnp.int32, (META, blk), 1)
    meta = jnp.zeros((META, blk), jnp.int32)
    for k in range(kmax):
        kept = jnp.logical_and(k < count, targets[k] == k)
        row = jnp.where(kept, aux_ref[k] * pb, PDEV)
        for n, value in enumerate((row, cols_ref[k] * blk)):
            meta = jnp.where(lanes == n * FIELD + k, value, meta)
    meta = meta.astype(jnp.float32).astype(jnp.bfloat16)
    split = kmax // 2 * pb
    for i in range(orbitals):
        half_ref[i, split : split + META, :] = meta

    for k in range(kmax):
        at = row_of(k, kmax, pb)

        @pl.when(k < count)
        def _(k=k, at=at):
            row = rows_ref[k]
            lane = pl.multiple_of(row % ao_blocks * blk, blk)
            occ = occ_ref[row // ao_blocks, :, pl.ds(lane, blk)].astype(jnp.float32)
            zero = jnp.zeros_like(occ)
            upper = jnp.concatenate([occ, zero], axis=1)
            lower = jnp.concatenate([zero, occ], axis=1)
            pair = jnp.concatenate([upper, lower], axis=0).astype(jnp.bfloat16)
            fetch(k).wait()
            stage = stage_ref.at[k]
            for p in range(0, pb, 2):
                rhs = tile_ref[k, p : p + 2].reshape(2 * blk, blk)
                part = jnp.dot(pair, rhs, preferred_element_type=jnp.float32)
                stage[p * orbitals : (p + 2) * orbitals, :] = part.astype(jnp.bfloat16).astype(
                    jnp.float32
                )
            for i in range(orbitals):
                half_ref[i, at : at + pb, :] = stage[
                    pl.ds(i, pb, stride=orbitals), :
                ].astype(jnp.bfloat16)

        if k:

            @pl.when(jnp.logical_and(k < count, targets[k] < k))
            def _(k=k):
                target = targets[k]
                total = stage_ref.at[target]
                total[...] += stage_ref[k]
                start = target * pb + jnp.where(target >= kmax // 2, META, 0)
                start = pl.multiple_of(start, META)
                for i in range(orbitals):
                    half_ref[i, pl.ds(start, pb), :] = total[
                        pl.ds(i, pb, stride=orbitals), :
                    ].astype(jnp.bfloat16)

        @pl.when(k >= count)
        def _(at=at):
            half_ref[:, at : at + pb, :] = jnp.zeros((orbitals, pb, blk), jnp.bfloat16)


def half_transform(tiles, rows, cols, auxs, count, occ):
    kmax, pb, blk, _ = tiles.shape
    orbitals = occ.shape[1]
    out = (orbitals, kmax * pb + META, blk)
    scalars = pl.BlockSpec(memory_space=pltpu.SMEM)
    return pl.pallas_call(
        half_kernel,
        in_specs=[scalars] * 4
        + [pl.BlockSpec(memory_space=pltpu.VMEM), pl.BlockSpec(memory_space=pl.ANY)],
        out_specs=pl.BlockSpec(memory_space=pltpu.VMEM),
        scratch_shapes=[
            pltpu.VMEM(tiles.shape, jnp.bfloat16),
            pltpu.VMEM((kmax, pb * orbitals, blk), jnp.float32),
            pltpu.SemaphoreType.DMA((kmax,)),
        ],
        out_shape=jax.ShapeDtypeStruct(out, jnp.bfloat16),
        compiler_params=pltpu.CompilerParams(vmem_limit_bytes=56 << 20),
        cost_estimate=pl.CostEstimate(
            flops=4 * tiles.size * orbitals, bytes_accessed=tiles.size * 2, transcendentals=0
        ),
        name="half_transform",
    )(rows, cols, auxs, count, occ, tiles)


def pair_kernel(kmax, pb, group, vb, kind, inputs, side, where_ref, *refs):
    half_refs, refs = refs[:inputs], refs[inputs:]
    vir_hbm, refs = refs[:group], refs[group:]
    vir_ref, dense_ref, sum_ref, turn_ref, meta_ref, code_ref, sem, sems = refs[-8:]
    results = refs[-8 - (2 if kind == "both" else 1) : -8]
    depth = vir_hbm[0].shape[0]
    blk = meta_ref.shape[1]
    low, high = columns_for(kind, vir_ref.shape[1] if kind == "both" else vir_hbm[0].shape[1], vb)
    fetches = [
        pltpu.make_async_copy(
            vir_hbm[d].at[:, pl.ds(low, high - low)], vir_ref.at[pl.ds(d * depth, depth), :], sems.at[d]
        )
        for d in range(group)
    ]
    for fetch in fetches:
        fetch.start()
    split = kmax // 2 * pb
    for g in range(group):
        meta_ref[g : g + 1, :] = (
            half_refs[0][g, split : split + META, :].astype(jnp.float32)[:1].astype(jnp.int32)
        )
    copy = pltpu.make_async_copy(meta_ref, code_ref, sem)
    copy.start()
    dense_ref[:PDEV, :] = jnp.zeros((PDEV, group * depth), jnp.bfloat16)
    copy.wait()

    def source(k):
        at = row_of(k, kmax, pb)
        if inputs == 2 and k >= kmax // 2:
            return half_refs[1], at - split - META
        return half_refs[0], at

    def scatter(step, carry):
        g = where_ref[2 + step]
        for k in range(kmax):
            ref, at = source(k)
            row = pl.multiple_of(code_ref[g, k], pb)
            lane = pl.multiple_of(step * depth + code_ref[g, FIELD + k], blk)
            dense_ref[pl.ds(row, pb), pl.ds(lane, blk)] = ref[g, at : at + pb, :]
        return carry

    lax.fori_loop(0, group, scatter, 0)
    for fetch in fetches:
        fetch.wait()
    sum_ref[...] = jnp.dot(dense_ref[:PDEV, :], vir_ref[...], preferred_element_type=jnp.float32)
    turn_ref[...] = sum_ref[...].T
    offset = 0
    if kind != "send":
        offset = vb
        column = pl.multiple_of(where_ref[side] * PDEV, PDEV)
        copy = pltpu.make_async_copy(
            turn_ref.at[:vb], results[-1].at[:, pl.ds(column, PDEV)], sems.at[group]
        )
        copy.start()
    if kind != "own":
        for j in range(results[0].shape[0]):
            results[0][j] = turn_ref[offset + j * vb : offset + (j + 1) * vb].astype(jnp.bfloat16)
    if kind != "send":
        copy.wait()


def columns_for(kind, width, vb):
    return {"both": (0, width), "own": (0, vb), "send": (vb, width)}[kind]


def pair_transform(kind, halves, virs, where, kmax, pb, vb, columns=0, result=None):
    group, _, blk = halves[0].shape
    depth, width = virs[0].shape
    others = width // vb - 1
    low, high = columns_for(kind, width, vb)
    anywhere = pl.BlockSpec(memory_space=pl.ANY)
    out_specs, out_shape = [], []
    if kind != "own":
        out_specs.append(whole((others, vb, PDEV)))
        out_shape.append(jax.ShapeDtypeStruct((others, vb, PDEV), jnp.bfloat16))
    if kind != "send":
        out_specs.append(anywhere)
        out_shape.append(jax.ShapeDtypeStruct((vb, columns), jnp.float32))
    return pl.pallas_call(
        functools.partial(pair_kernel, kmax, pb, group, vb, kind, len(halves), int(result is not None)),
        grid_spec=pltpu.PrefetchScalarGridSpec(
            num_scalar_prefetch=1,
            grid=(1,),
            in_specs=[whole(x.shape) for x in halves] + [anywhere] * (group + (result is not None)),
            out_specs=out_specs,
            scratch_shapes=[
                pltpu.VMEM((group * depth, high - low), jnp.bfloat16),
                pltpu.VMEM((PDEV + pb, group * depth), jnp.bfloat16),
                pltpu.VMEM((PDEV, high - low), jnp.float32),
                pltpu.VMEM((high - low, PDEV), jnp.float32),
                pltpu.VMEM((group, blk), jnp.int32),
                pltpu.SMEM((group, blk), jnp.int32),
                pltpu.SemaphoreType.DMA,
                pltpu.SemaphoreType.DMA((group + 1,)),
            ],
        ),
        out_shape=out_shape,
        input_output_aliases={} if result is None else {1 + len(halves) + group: 0},
        compiler_params=pltpu.CompilerParams(vmem_limit_bytes=PAIR_LIMIT << 20),
        cost_estimate=pl.CostEstimate(
            flops=4 * PDEV * group * depth * (high - low),
            bytes_accessed=group * depth * (high - low) * 2 + halves[0].size * 2,
            transcendentals=0,
        ),
        name=kind + "_part",
    )(where, *halves, *virs, *([] if result is None else [result]))


def place_kernel(side, where_ref, got_ref, _, out_hbm, wide_ref, sems):
    copies = []
    for j in range(got_ref.shape[0]):
        wide_ref[j] = got_ref[j].astype(jnp.float32)
        block = jnp.bitwise_xor(where_ref[side], 2 * (j + 1))
        lane = pl.multiple_of(block * PDEV, PDEV)
        copies.append(pltpu.make_async_copy(wide_ref.at[j], out_hbm.at[:, pl.ds(lane, PDEV)], sems.at[j]))
        copies[-1].start()
    for copy in copies:
        copy.wait()


def place(where, got, result, side):
    return pl.pallas_call(
        functools.partial(place_kernel, side),
        grid_spec=pltpu.PrefetchScalarGridSpec(
            num_scalar_prefetch=1,
            grid=(1,),
            in_specs=[whole(got.shape), pl.BlockSpec(memory_space=pl.ANY)],
            out_specs=pl.BlockSpec(memory_space=pl.ANY),
            scratch_shapes=[
                pltpu.VMEM(got.shape, jnp.float32),
                pltpu.SemaphoreType.DMA((got.shape[0],)),
            ],
        ),
        out_shape=jax.ShapeDtypeStruct(result.shape, jnp.float32),
        input_output_aliases={2: 0},
        cost_estimate=pl.CostEstimate(flops=0, bytes_accessed=got.size * 6, transcendentals=0),
        compiler_params=pltpu.CompilerParams(vmem_limit_bytes=PLACE_LIMIT << 20),
        name="place",
    )(where, got, result)


def open_kernel(vb, vir_hbm, occ_ref, occ_out_ref, out_ref, sems):
    aux = lax.axis_index("aux")
    copies = []
    for j in range(out_ref.shape[1] // vb):
        block = jnp.bitwise_xor(aux // 2, j) * 2 + aux % 2
        copies.append(
            pltpu.make_async_copy(
                vir_hbm.at[:, pl.ds(pl.multiple_of(block * vb, vb), vb)],
                out_ref.at[:, pl.ds(j * vb, vb)],
                sems.at[j],
            )
        )
        copies[-1].start()
    occ_out_ref[...] = jnp.broadcast_to(occ_ref[...][None], occ_out_ref.shape)
    for copy in copies:
        copy.wait()


def opening(vir, occ, group_size, aux, aux_size, vb):
    rows = vir.shape[0]
    parts = aux_size // 2
    copies = (group_size, *occ.shape)
    if vb % 128:
        order = jnp.bitwise_xor(aux // 2, jnp.arange(parts)) * 2 + aux % 2
        chosen = jnp.take(vir.reshape(rows, aux_size, vb), order, axis=1)
        return jnp.broadcast_to(occ[None], copies), chosen.reshape(rows, -1)
    vmem = pl.BlockSpec(memory_space=pltpu.VMEM)
    return pl.pallas_call(
        functools.partial(open_kernel, vb),
        in_specs=[pl.BlockSpec(memory_space=pl.ANY), vmem],
        out_specs=[vmem, vmem],
        scratch_shapes=[pltpu.SemaphoreType.DMA((parts,))],
        out_shape=[
            jax.ShapeDtypeStruct(copies, occ.dtype),
            jax.ShapeDtypeStruct((rows, parts * vb), vir.dtype),
        ],
        compiler_params=pltpu.CompilerParams(vmem_limit_bytes=60 << 20),
        name="opening",
    )(vir, occ)


def shards(integral_tiles, row_blocks, col_blocks, aux_blocks, tile_counts, occ_coeffs, vir_coeffs):
    group_size = lax.axis_size("grp")
    aux_size = lax.axis_size("aux")
    aux = lax.axis_index("aux")
    kmax, pb = integral_tiles.shape[2:4]
    orbitals = occ_coeffs.shape[0]
    virtuals = vir_coeffs.shape[1]
    vb = virtuals * orbitals // (group_size * aux_size)

    def swap(x, step):
        return lax.ppermute(x, "aux", [(a, a ^ step) for a in range(aux_size)])

    def hop(x, steps):
        return lax.ppermute(x, "grp", [(g, g ^ steps[g % 2]) for g in range(group_size)])

    occ, own = opening(vir_coeffs, occ_coeffs, group_size, aux, aux_size, vb)
    occ = lax.all_to_all(occ, "grp", split_axis=0, concat_axis=0, tiled=True)

    core = lax.axis_index("grp") % 2
    near = hop(own, (2, 4))
    far = hop(own, (4, 2))
    occ, near = lax.optimization_barrier((occ, near))
    across = hop(near, (4, 2))
    halves = half_transform(
        integral_tiles[0, 0], row_blocks[0, 0], col_blocks[0, 0], aux_blocks[0, 0], tile_counts[0], occ
    )
    others = swap(halves, 1)
    halves, far, across = lax.optimization_barrier((halves, far, across))
    virs = [own, near, far, across]
    virs = virs + [hop(vir, (1, 1)) for vir in virs]

    halves = lax.all_to_all(halves, "grp", split_axis=0, concat_axis=0, tiled=True)
    others, halves = lax.optimization_barrier((others, halves))
    others = lax.all_to_all(others, "grp", split_axis=0, concat_axis=0, tiled=True)

    moved = [0, 2 + 2 * core, 4 - 2 * core, 6, 1, 5 - 2 * core, 3 + 2 * core, 7]
    moved = [jnp.bitwise_xor(lax.axis_index("grp"), step) for step in moved]
    where = jnp.stack([aux, jnp.bitwise_xor(aux, 1)] + moved).astype(jnp.int32)

    def trade(send):
        if aux_size == 4:
            return swap(send, 2)
        return jnp.stack([swap(send[j - 1], 2 * j) for j in range(1, aux_size // 2)])

    sizes = (kmax, pb, vb)
    columns = aux_size * PDEV
    if vb % 128:
        send_first, result = pair_transform("both", [halves], virs, where, *sizes, columns=columns)
        send_second, own_second = pair_transform("both", [others], virs, where, *sizes, columns=columns)
        got_first = trade(send_first)
        block = (jnp.bitwise_xor(aux, 1) * PDEV).astype(jnp.int32)
        own_second = lax.dynamic_slice_in_dim(own_second, (aux * PDEV).astype(jnp.int32), PDEV, 1)
        result = lax.dynamic_update_slice_in_dim(result, own_second, block, 1)
    else:
        (send_first,) = pair_transform("send", [halves], virs, where, *sizes)
        got_first = trade(send_first)
        others, _ = lax.optimization_barrier((others, send_first))
        (send_second,) = pair_transform("send", [others], virs, where, *sizes)
        others, halves, _ = lax.optimization_barrier((others, halves, send_second))
        (result,) = pair_transform("own", [halves], virs, where, *sizes, columns=columns)
        (result,) = pair_transform("own", [others], virs, where, *sizes, columns=columns, result=result)
    result = place(where, got_first, result, 0)
    return place(where, trade(send_second), result, 1)


def solution(mesh):
    in_specs = (
        P("grp", "aux", None, None, None, None),
        P("grp", "aux", None),
        P("grp", "aux", None),
        P("grp", "aux", None),
        P("grp", "aux"),
        P(None, "grp"),
        P("grp", None),
    )
    out_specs = P(("grp", "aux"), None)
    return jax.shard_map(shards, mesh=mesh, in_specs=in_specs, out_specs=out_specs, check_vma=False)
```

```python
import functools

import jax
import jax.numpy as jnp
from jax import lax
from jax.experimental import pallas as pl
from jax.experimental.pallas import tpu as pltpu
from jax.sharding import PartitionSpec as P

PDEV = 512
META = 16
PAIR_LIMIT = 40
PLACE_LIMIT = 40
FIELD = 16


def whole(shape):
    return pl.BlockSpec(shape, lambda n, *_: (0,) * len(shape))


def row_of(k, kmax, pb):
    return k * pb + (META if k >= kmax // 2 else 0)


def half_kernel(rows_ref, cols_ref, aux_ref, count_ref, occ_hbm, tiles_hbm, half_ref, occ_ref, tile_ref, stage_ref, sems):
    kmax, pb, blk, _ = tile_ref.shape
    orbitals = half_ref.shape[0]
    ao_blocks = occ_ref.shape[2] // blk
    count = count_ref[0]

    def fetch(k):
        return pltpu.make_async_copy(tiles_hbm.at[k], tile_ref.at[k], sems.at[k])

    fetch_occ = pltpu.make_async_copy(occ_hbm, occ_ref, sems.at[kmax])
    fetch_occ.start()
    for k in range(kmax):

        @pl.when(k < count)
        def _():
            fetch(k).start()

    targets = []
    for k in range(kmax):
        target = jnp.int32(k)
        for j in reversed(range(k)):
            same = jnp.logical_and(cols_ref[j] == cols_ref[k], aux_ref[j] == aux_ref[k])
            target = jnp.where(same, j, target)
        targets.append(target)
    lanes = lax.broadcasted_iota(jnp.int32, (META, blk), 1)
    meta = jnp.zeros((META, blk), jnp.int32)
    for k in range(kmax):
        kept = jnp.logical_and(k < count, targets[k] == k)
        row = jnp.where(kept, aux_ref[k] * pb, PDEV)
        for n, value in enumerate((row, cols_ref[k] * blk)):
            meta = jnp.where(lanes == n * FIELD + k, value, meta)
    meta = meta.astype(jnp.float32).astype(jnp.bfloat16)
    split = kmax // 2 * pb
    for i in range(orbitals):
        half_ref[i, split : split + META, :] = meta
    fetch_occ.wait()

    for k in range(kmax):
        at = row_of(k, kmax, pb)

        @pl.when(k < count)
        def _(k=k, at=at):
            row = rows_ref[k]
            lane = pl.multiple_of(row % ao_blocks * blk, blk)
            occ = occ_ref[row // ao_blocks, :, pl.ds(lane, blk)].astype(jnp.float32)
            zero = jnp.zeros_like(occ)
            upper = jnp.concatenate([occ, zero], axis=1)
            lower = jnp.concatenate([zero, occ], axis=1)
            pair = jnp.concatenate([upper, lower], axis=0).astype(jnp.bfloat16)
            fetch(k).wait()
            stage = stage_ref.at[k]
            for p in range(0, pb, 2):
                rhs = tile_ref[k, p : p + 2].reshape(2 * blk, blk)
                part = jnp.dot(pair, rhs, preferred_element_type=jnp.float32)
                stage[p * orbitals : (p + 2) * orbitals, :] = part.astype(jnp.bfloat16).astype(
                    jnp.float32
                )
            for i in range(orbitals):
                half_ref[i, at : at + pb, :] = stage[
                    pl.ds(i, pb, stride=orbitals), :
                ].astype(jnp.bfloat16)

        if k:

            @pl.when(jnp.logical_and(k < count, targets[k] < k))
            def _(k=k):
                target = targets[k]
                total = stage_ref.at[target]
                total[...] += stage_ref[k]
                start = target * pb + jnp.where(target >= kmax // 2, META, 0)
                start = pl.multiple_of(start, META)
                for i in range(orbitals):
                    half_ref[i, pl.ds(start, pb), :] = total[
                        pl.ds(i, pb, stride=orbitals), :
                    ].astype(jnp.bfloat16)

        @pl.when(k >= count)
        def _(at=at):
            half_ref[:, at : at + pb, :] = jnp.zeros((orbitals, pb, blk), jnp.bfloat16)


def half_transform(tiles, rows, cols, auxs, count, occ):
    kmax, pb, blk, _ = tiles.shape
    orbitals = occ.shape[1]
    out = (orbitals, kmax * pb + META, blk)
    scalars = pl.BlockSpec(memory_space=pltpu.SMEM)
    return pl.pallas_call(
        half_kernel,
        in_specs=[scalars] * 4
        + [pl.BlockSpec(memory_space=pl.ANY)] * 2,
        out_specs=pl.BlockSpec(memory_space=pltpu.VMEM),
        scratch_shapes=[
            pltpu.VMEM(occ.shape, jnp.bfloat16),
            pltpu.VMEM(tiles.shape, jnp.bfloat16),
            pltpu.VMEM((kmax, pb * orbitals, blk), jnp.float32),
            pltpu.SemaphoreType.DMA((kmax + 1,)),
        ],
        out_shape=jax.ShapeDtypeStruct(out, jnp.bfloat16),
        compiler_params=pltpu.CompilerParams(vmem_limit_bytes=63 << 20),
        cost_estimate=pl.CostEstimate(
            flops=160 * tiles.size * orbitals, bytes_accessed=tiles.size * 80, transcendentals=0
        ),
        name="half_transform",
    )(rows, cols, auxs, count, occ, tiles)


def pair_kernel(kmax, pb, group, vb, kind, inputs, side, where_ref, *refs):
    half_refs, refs = refs[:inputs], refs[inputs:]
    vir_hbm, refs = refs[:group], refs[group:]
    vir_ref, dense_ref, sum_ref, turn_ref, meta_ref, code_ref, sem, sems = refs[-8:]
    results = refs[-8 - (2 if kind == "both" else 1) : -8]
    depth = vir_hbm[0].shape[0]
    blk = meta_ref.shape[1]
    low, high = columns_for(kind, vir_ref.shape[1] if kind == "both" else vir_hbm[0].shape[1], vb)
    fetches = [
        pltpu.make_async_copy(
            vir_hbm[d].at[:, pl.ds(low, high - low)], vir_ref.at[pl.ds(d * depth, depth), :], sems.at[d]
        )
        for d in range(group)
    ]
    for fetch in fetches:
        fetch.start()
    split = kmax // 2 * pb
    for g in range(group):
        meta_ref[g : g + 1, :] = (
            half_refs[0][g, split : split + META, :].astype(jnp.float32)[:1].astype(jnp.int32)
        )
    copy = pltpu.make_async_copy(meta_ref, code_ref, sem)
    copy.start()
    dense_ref[:PDEV, :] = jnp.zeros((PDEV, group * depth), jnp.bfloat16)
    copy.wait()

    def source(k):
        at = row_of(k, kmax, pb)
        if inputs == 2 and k >= kmax // 2:
            return half_refs[1], at - split - META
        return half_refs[0], at

    def scatter(step, carry):
        g = where_ref[2 + step]
        for k in range(kmax):
            ref, at = source(k)
            row = pl.multiple_of(code_ref[g, k], pb)
            lane = pl.multiple_of(step * depth + code_ref[g, FIELD + k], blk)
            dense_ref[pl.ds(row, pb), pl.ds(lane, blk)] = ref[g, at : at + pb, :]
        return carry

    lax.fori_loop(0, group, scatter, 0)
    for fetch in fetches:
        fetch.wait()
    sum_ref[...] = jnp.dot(dense_ref[:PDEV, :], vir_ref[...], preferred_element_type=jnp.float32)
    turn_ref[...] = sum_ref[...].T
    offset = 0
    if kind != "send":
        offset = vb
        column = pl.multiple_of(where_ref[side] * PDEV, PDEV)
        copy = pltpu.make_async_copy(
            turn_ref.at[:vb], results[-1].at[:, pl.ds(column, PDEV)], sems.at[group]
        )
        copy.start()
    if kind != "own":
        for j in range(results[0].shape[0]):
            results[0][j] = turn_ref[offset + j * vb : offset + (j + 1) * vb].astype(jnp.bfloat16)
    if kind != "send":
        copy.wait()


def columns_for(kind, width, vb):
    return {"both": (0, width), "own": (0, vb), "send": (vb, width)}[kind]


def pair_transform(kind, halves, virs, where, kmax, pb, vb, columns=0, result=None):
    group, _, blk = halves[0].shape
    depth, width = virs[0].shape
    others = width // vb - 1
    low, high = columns_for(kind, width, vb)
    anywhere = pl.BlockSpec(memory_space=pl.ANY)
    out_specs, out_shape = [], []
    if kind != "own":
        out_specs.append(whole((others, vb, PDEV)))
        out_shape.append(jax.ShapeDtypeStruct((others, vb, PDEV), jnp.bfloat16))
    if kind != "send":
        out_specs.append(anywhere)
        out_shape.append(jax.ShapeDtypeStruct((vb, columns), jnp.float32))
    return pl.pallas_call(
        functools.partial(pair_kernel, kmax, pb, group, vb, kind, len(halves), int(result is not None)),
        grid_spec=pltpu.PrefetchScalarGridSpec(
            num_scalar_prefetch=1,
            grid=(1,),
            in_specs=[whole(x.shape) for x in halves] + [anywhere] * (group + (result is not None)),
            out_specs=out_specs,
            scratch_shapes=[
                pltpu.VMEM((group * depth, high - low), jnp.bfloat16),
                pltpu.VMEM((PDEV + pb, group * depth), jnp.bfloat16),
                pltpu.VMEM((PDEV, high - low), jnp.float32),
                pltpu.VMEM((high - low, PDEV), jnp.float32),
                pltpu.VMEM((group, blk), jnp.int32),
                pltpu.SMEM((group, blk), jnp.int32),
                pltpu.SemaphoreType.DMA,
                pltpu.SemaphoreType.DMA((group + 1,)),
            ],
        ),
        out_shape=out_shape,
        input_output_aliases={} if result is None else {1 + len(halves) + group: 0},
        compiler_params=pltpu.CompilerParams(vmem_limit_bytes=PAIR_LIMIT << 20),
        cost_estimate=pl.CostEstimate(
            flops=4 * PDEV * group * depth * (high - low),
            bytes_accessed=group * depth * (high - low) * 2 + halves[0].size * 2,
            transcendentals=0,
        ),
        name=kind + "_part",
    )(where, *halves, *virs, *([] if result is None else [result]))


def place_kernel(side, where_ref, got_ref, _, out_hbm, wide_ref, sems):
    copies = []
    for j in range(got_ref.shape[0]):
        wide_ref[j] = got_ref[j].astype(jnp.float32)
        block = jnp.bitwise_xor(where_ref[side], 2 * (j + 1))
        lane = pl.multiple_of(block * PDEV, PDEV)
        copies.append(pltpu.make_async_copy(wide_ref.at[j], out_hbm.at[:, pl.ds(lane, PDEV)], sems.at[j]))
        copies[-1].start()
    for copy in copies:
        copy.wait()


def place(where, got, result, side):
    return pl.pallas_call(
        functools.partial(place_kernel, side),
        grid_spec=pltpu.PrefetchScalarGridSpec(
            num_scalar_prefetch=1,
            grid=(1,),
            in_specs=[whole(got.shape), pl.BlockSpec(memory_space=pl.ANY)],
            out_specs=pl.BlockSpec(memory_space=pl.ANY),
            scratch_shapes=[
                pltpu.VMEM(got.shape, jnp.float32),
                pltpu.SemaphoreType.DMA((got.shape[0],)),
            ],
        ),
        out_shape=jax.ShapeDtypeStruct(result.shape, jnp.float32),
        input_output_aliases={2: 0},
        cost_estimate=pl.CostEstimate(flops=0, bytes_accessed=got.size * 6, transcendentals=0),
        compiler_params=pltpu.CompilerParams(vmem_limit_bytes=PLACE_LIMIT << 20),
        name="place",
    )(where, got, result)


def open_kernel(vb, vir_hbm, occ_hbm, occ_out_hbm, out_hbm, vir_ref, occ_ref, in_sems, out_sems):
    aux = lax.axis_index("aux")
    parts = out_hbm.shape[1] // vb
    fetch_occ = pltpu.make_async_copy(occ_hbm, occ_ref, in_sems.at[parts])
    fetch_occ.start()
    fetches = []
    for j in range(parts):
        block = jnp.bitwise_xor(aux // 2, j) * 2 + aux % 2
        fetches.append(
            pltpu.make_async_copy(
                vir_hbm.at[:, pl.ds(pl.multiple_of(block * vb, vb), vb)], vir_ref.at[j], in_sems.at[j]
            )
        )
        fetches[-1].start()
    stores = [
        pltpu.make_async_copy(vir_ref.at[j], out_hbm.at[:, pl.ds(j * vb, vb)], out_sems.at[j])
        for j in range(parts)
    ]
    fetch_occ.wait()
    for g in range(occ_out_hbm.shape[0]):
        stores.append(pltpu.make_async_copy(occ_ref, occ_out_hbm.at[g], out_sems.at[parts + g]))
        stores[-1].start()
    for j in range(parts):
        fetches[j].wait()
        stores[j].start()
    for store in stores:
        store.wait()


def opening(vir, occ, group_size, aux, aux_size, vb):
    rows = vir.shape[0]
    parts = aux_size // 2
    copies = (group_size, *occ.shape)
    if vb % 128:
        order = jnp.bitwise_xor(aux // 2, jnp.arange(parts)) * 2 + aux % 2
        chosen = jnp.take(vir.reshape(rows, aux_size, vb), order, axis=1)
        return jnp.broadcast_to(occ[None], copies), chosen.reshape(rows, -1)
    anywhere = pl.BlockSpec(memory_space=pl.ANY)
    return pl.pallas_call(
        functools.partial(open_kernel, vb),
        in_specs=[anywhere] * 2,
        out_specs=[anywhere] * 2,
        scratch_shapes=[
            pltpu.VMEM((parts, rows, vb), vir.dtype),
            pltpu.VMEM(occ.shape, occ.dtype),
            pltpu.SemaphoreType.DMA((parts + 1,)),
            pltpu.SemaphoreType.DMA((parts + group_size,)),
        ],
        out_shape=[
            jax.ShapeDtypeStruct(copies, occ.dtype),
            jax.ShapeDtypeStruct((rows, parts * vb), vir.dtype),
        ],
        compiler_params=pltpu.CompilerParams(vmem_limit_bytes=63 << 20),
        name="opening",
    )(vir, occ)


def shards(integral_tiles, row_blocks, col_blocks, aux_blocks, tile_counts, occ_coeffs, vir_coeffs):
    group_size = lax.axis_size("grp")
    aux_size = lax.axis_size("aux")
    aux = lax.axis_index("aux")
    kmax, pb = integral_tiles.shape[2:4]
    orbitals = occ_coeffs.shape[0]
    virtuals = vir_coeffs.shape[1]
    vb = virtuals * orbitals // (group_size * aux_size)

    def swap(x, step):
        return lax.ppermute(x, "aux", [(a, a ^ step) for a in range(aux_size)])

    def hop(x, steps):
        return lax.ppermute(x, "grp", [(g, g ^ steps[g % 2]) for g in range(group_size)])

    occ, own = opening(vir_coeffs, occ_coeffs, group_size, aux, aux_size, vb)
    occ = lax.all_to_all(occ, "grp", split_axis=0, concat_axis=0, tiled=True)

    core = lax.axis_index("grp") % 2
    near = hop(own, (2, 4))
    far = hop(own, (4, 2))
    across = hop(near, (4, 2))
    halves = half_transform(
        integral_tiles[0, 0], row_blocks[0, 0], col_blocks[0, 0], aux_blocks[0, 0], tile_counts[0], occ
    )
    others = swap(halves, 1)
    halves, far, across = lax.optimization_barrier((halves, far, across))
    virs = [own, near, far, across]
    virs = virs + [hop(vir, (1, 1)) for vir in virs]

    halves = lax.all_to_all(halves, "grp", split_axis=0, concat_axis=0, tiled=True)
    others, halves = lax.optimization_barrier((others, halves))
    others = lax.all_to_all(others, "grp", split_axis=0, concat_axis=0, tiled=True)

    moved = [0, 2 + 2 * core, 4 - 2 * core, 6, 1, 5 - 2 * core, 3 + 2 * core, 7]
    moved = [jnp.bitwise_xor(lax.axis_index("grp"), step) for step in moved]
    where = jnp.stack([aux, jnp.bitwise_xor(aux, 1)] + moved).astype(jnp.int32)

    def trade(send):
        if aux_size == 4:
            return swap(send, 2)
        return jnp.stack([swap(send[j - 1], 2 * j) for j in range(1, aux_size // 2)])

    sizes = (kmax, pb, vb)
    columns = aux_size * PDEV
    if vb % 128:
        send_first, result = pair_transform("both", [halves], virs, where, *sizes, columns=columns)
        send_second, own_second = pair_transform("both", [others], virs, where, *sizes, columns=columns)
        got_first = trade(send_first)
        block = (jnp.bitwise_xor(aux, 1) * PDEV).astype(jnp.int32)
        own_second = lax.dynamic_slice_in_dim(own_second, (aux * PDEV).astype(jnp.int32), PDEV, 1)
        result = lax.dynamic_update_slice_in_dim(result, own_second, block, 1)
    else:
        (send_first,) = pair_transform("send", [halves], virs, where, *sizes)
        got_first = trade(send_first)
        others, _ = lax.optimization_barrier((others, send_first))
        (send_second,) = pair_transform("send", [others], virs, where, *sizes)
        others, halves, _ = lax.optimization_barrier((others, halves, send_second))
        (result,) = pair_transform("own", [halves], virs, where, *sizes, columns=columns)
        (result,) = pair_transform("own", [others], virs, where, *sizes, columns=columns, result=result)
    result = place(where, got_first, result, 0)
    return place(where, trade(send_second), result, 1)


def solution(mesh):
    in_specs = (
        P("grp", "aux", None, None, None, None),
        P("grp", "aux", None),
        P("grp", "aux", None),
        P("grp", "aux", None),
        P("grp", "aux"),
        P(None, "grp"),
        P("grp", None),
    )
    out_specs = P(("grp", "aux"), None)
    return jax.shard_map(shards, mesh=mesh, in_specs=in_specs, out_specs=out_specs, check_vma=False)
```

```python
import functools

import jax
import jax.numpy as jnp
from jax import lax
from jax.experimental import pallas as pl
from jax.experimental.pallas import tpu as pltpu
from jax.sharding import PartitionSpec as P

PDEV = 512
META = 16
PIECES = 4
PAIR_LIMIT = 40
PLACE_LIMIT = 40
FIELD = 16


def whole(shape):
    return pl.BlockSpec(shape, lambda n, *_: (0,) * len(shape))


def row_of(k, kmax, pb):
    return k * pb + (META if k >= kmax // 2 else 0)


def half_kernel(rows_ref, cols_ref, aux_ref, count_ref, occ_hbm, tiles_hbm, half_ref, occ_ref, tile_ref, stage_ref, sems):
    kmax, pb, blk, _ = tile_ref.shape
    orbitals = half_ref.shape[0]
    ao_blocks = occ_ref.shape[2] // blk
    count = count_ref[0]

    def fetch(k):
        return pltpu.make_async_copy(tiles_hbm.at[k], tile_ref.at[k], sems.at[k])

    fetch_occ = pltpu.make_async_copy(occ_hbm, occ_ref, sems.at[kmax])
    fetch_occ.start()
    for k in range(kmax):

        @pl.when(k < count)
        def _():
            fetch(k).start()

    targets = []
    for k in range(kmax):
        target = jnp.int32(k)
        for j in reversed(range(k)):
            same = jnp.logical_and(cols_ref[j] == cols_ref[k], aux_ref[j] == aux_ref[k])
            target = jnp.where(same, j, target)
        targets.append(target)
    lanes = lax.broadcasted_iota(jnp.int32, (META, blk), 1)
    meta = jnp.zeros((META, blk), jnp.int32)
    for k in range(kmax):
        kept = jnp.logical_and(k < count, targets[k] == k)
        row = jnp.where(kept, aux_ref[k] * pb, PDEV)
        for n, value in enumerate((row, cols_ref[k] * blk)):
            meta = jnp.where(lanes == n * FIELD + k, value, meta)
    meta = meta.astype(jnp.float32).astype(jnp.bfloat16)
    split = kmax // 2 * pb
    for i in range(orbitals):
        half_ref[i, split : split + META, :] = meta
    fetch_occ.wait()

    for k in range(kmax):
        at = row_of(k, kmax, pb)

        @pl.when(k < count)
        def _(k=k, at=at):
            row = rows_ref[k]
            lane = pl.multiple_of(row % ao_blocks * blk, blk)
            occ = occ_ref[row // ao_blocks, :, pl.ds(lane, blk)].astype(jnp.float32)
            zero = jnp.zeros_like(occ)
            upper = jnp.concatenate([occ, zero], axis=1)
            lower = jnp.concatenate([zero, occ], axis=1)
            pair = jnp.concatenate([upper, lower], axis=0).astype(jnp.bfloat16)
            fetch(k).wait()
            stage = stage_ref.at[k]
            for p in range(0, pb, 2):
                rhs = tile_ref[k, p : p + 2].reshape(2 * blk, blk)
                part = jnp.dot(pair, rhs, preferred_element_type=jnp.float32)
                stage[p * orbitals : (p + 2) * orbitals, :] = part.astype(jnp.bfloat16).astype(
                    jnp.float32
                )
            for i in range(orbitals):
                half_ref[i, at : at + pb, :] = stage[
                    pl.ds(i, pb, stride=orbitals), :
                ].astype(jnp.bfloat16)

        if k:

            @pl.when(jnp.logical_and(k < count, targets[k] < k))
            def _(k=k):
                target = targets[k]
                total = stage_ref.at[target]
                total[...] += stage_ref[k]
                start = target * pb + jnp.where(target >= kmax // 2, META, 0)
                start = pl.multiple_of(start, META)
                for i in range(orbitals):
                    half_ref[i, pl.ds(start, pb), :] = total[
                        pl.ds(i, pb, stride=orbitals), :
                    ].astype(jnp.bfloat16)

        @pl.when(k >= count)
        def _(at=at):
            half_ref[:, at : at + pb, :] = jnp.zeros((orbitals, pb, blk), jnp.bfloat16)


def half_transform(tiles, rows, cols, auxs, count, occ):
    kmax, pb, blk, _ = tiles.shape
    orbitals = occ.shape[1]
    out = (orbitals, kmax * pb + META, blk)
    scalars = pl.BlockSpec(memory_space=pltpu.SMEM)
    return pl.pallas_call(
        half_kernel,
        in_specs=[scalars] * 4
        + [pl.BlockSpec(memory_space=pl.ANY)] * 2,
        out_specs=pl.BlockSpec(memory_space=pltpu.VMEM),
        scratch_shapes=[
            pltpu.VMEM(occ.shape, jnp.bfloat16),
            pltpu.VMEM(tiles.shape, jnp.bfloat16),
            pltpu.VMEM((kmax, pb * orbitals, blk), jnp.float32),
            pltpu.SemaphoreType.DMA((kmax + 1,)),
        ],
        out_shape=jax.ShapeDtypeStruct(out, jnp.bfloat16),
        compiler_params=pltpu.CompilerParams(vmem_limit_bytes=63 << 20),
        cost_estimate=pl.CostEstimate(
            flops=160 * tiles.size * orbitals, bytes_accessed=tiles.size * 80, transcendentals=0
        ),
        name="half_transform",
    )(rows, cols, auxs, count, occ, tiles)


def pair_kernel(kmax, pb, group, vb, kind, inputs, side, where_ref, *refs):
    half_refs, refs = refs[:inputs], refs[inputs:]
    vir_hbm, refs = refs[:group], refs[group:]
    vir_ref, dense_ref, sum_ref, turn_ref, meta_ref, code_ref, sem, sems = refs[-8:]
    results = refs[-8 - (2 if kind == "both" else 1) : -8]
    depth = vir_hbm[0].shape[0]
    blk = meta_ref.shape[1]
    low, high = columns_for(kind, vir_ref.shape[1] if kind == "both" else vir_hbm[0].shape[1], vb)
    fetches = [
        pltpu.make_async_copy(
            vir_hbm[d].at[:, pl.ds(low, high - low)], vir_ref.at[pl.ds(d * depth, depth), :], sems.at[d]
        )
        for d in range(group)
    ]
    for fetch in fetches:
        fetch.start()
    split = kmax // 2 * pb
    for g in range(group):
        meta_ref[g : g + 1, :] = (
            half_refs[0][g, split : split + META, :].astype(jnp.float32)[:1].astype(jnp.int32)
        )
    copy = pltpu.make_async_copy(meta_ref, code_ref, sem)
    copy.start()
    dense_ref[:PDEV, :] = jnp.zeros((PDEV, group * depth), jnp.bfloat16)
    copy.wait()

    def source(k):
        at = row_of(k, kmax, pb)
        if inputs == 2 and k >= kmax // 2:
            return half_refs[1], at - split - META
        return half_refs[0], at

    def scatter(step, carry):
        g = where_ref[2 + step]
        for k in range(kmax):
            ref, at = source(k)
            row = pl.multiple_of(code_ref[g, k], pb)
            lane = pl.multiple_of(step * depth + code_ref[g, FIELD + k], blk)
            dense_ref[pl.ds(row, pb), pl.ds(lane, blk)] = ref[g, at : at + pb, :]
        return carry

    lax.fori_loop(0, group, scatter, 0)
    for fetch in fetches:
        fetch.wait()
    sum_ref[...] = jnp.dot(dense_ref[:PDEV, :], vir_ref[...], preferred_element_type=jnp.float32)
    turn_ref[...] = sum_ref[...].T
    offset = 0
    if kind != "send":
        offset = vb
        column = pl.multiple_of(where_ref[side] * PDEV, PDEV)
        copy = pltpu.make_async_copy(
            turn_ref.at[:vb], results[-1].at[:, pl.ds(column, PDEV)], sems.at[group]
        )
        copy.start()
    if kind != "own":
        for j in range(results[0].shape[0]):
            results[0][j] = turn_ref[offset + j * vb : offset + (j + 1) * vb].astype(jnp.bfloat16)
    if kind != "send":
        copy.wait()


def columns_for(kind, width, vb):
    return {"both": (0, width), "own": (0, vb), "send": (vb, width)}[kind]


def pair_transform(kind, halves, virs, where, kmax, pb, vb, columns=0, result=None):
    group, _, blk = halves[0].shape
    depth, width = virs[0].shape
    others = width // vb - 1
    low, high = columns_for(kind, width, vb)
    anywhere = pl.BlockSpec(memory_space=pl.ANY)
    out_specs, out_shape = [], []
    if kind != "own":
        out_specs.append(whole((others, vb, PDEV)))
        out_shape.append(jax.ShapeDtypeStruct((others, vb, PDEV), jnp.bfloat16))
    if kind != "send":
        out_specs.append(anywhere)
        out_shape.append(jax.ShapeDtypeStruct((vb, columns), jnp.float32))
    return pl.pallas_call(
        functools.partial(pair_kernel, kmax, pb, group, vb, kind, len(halves), int(result is not None)),
        grid_spec=pltpu.PrefetchScalarGridSpec(
            num_scalar_prefetch=1,
            grid=(1,),
            in_specs=[whole(x.shape) for x in halves] + [anywhere] * (group + (result is not None)),
            out_specs=out_specs,
            scratch_shapes=[
                pltpu.VMEM((group * depth, high - low), jnp.bfloat16),
                pltpu.VMEM((PDEV + pb, group * depth), jnp.bfloat16),
                pltpu.VMEM((PDEV, high - low), jnp.float32),
                pltpu.VMEM((high - low, PDEV), jnp.float32),
                pltpu.VMEM((group, blk), jnp.int32),
                pltpu.SMEM((group, blk), jnp.int32),
                pltpu.SemaphoreType.DMA,
                pltpu.SemaphoreType.DMA((group + 1,)),
            ],
        ),
        out_shape=out_shape,
        input_output_aliases={} if result is None else {1 + len(halves) + group: 0},
        compiler_params=pltpu.CompilerParams(vmem_limit_bytes=PAIR_LIMIT << 20),
        cost_estimate=pl.CostEstimate(
            flops=4 * PDEV * group * depth * (high - low),
            bytes_accessed=group * depth * (high - low) * 2 + halves[0].size * 2,
            transcendentals=0,
        ),
        name=kind + "_part",
    )(where, *halves, *virs, *([] if result is None else [result]))


def place_kernel(side, where_ref, got_ref, _, out_hbm, wide_ref, sems):
    copies = []
    piece = got_ref.shape[1] // PIECES
    for j in range(got_ref.shape[0]):
        block = jnp.bitwise_xor(where_ref[side], 2 * (j + 1))
        lane = pl.multiple_of(block * PDEV, PDEV)
        for n in range(PIECES):
            rows = pl.ds(n * piece, piece)
            wide_ref[j, rows, :] = got_ref[j, rows, :].astype(jnp.float32)
            copies.append(
                pltpu.make_async_copy(
                    wide_ref.at[j, rows], out_hbm.at[rows, pl.ds(lane, PDEV)], sems.at[j * PIECES + n]
                )
            )
            copies[-1].start()
    for copy in copies:
        copy.wait()


def place(where, got, result, side):
    return pl.pallas_call(
        functools.partial(place_kernel, side),
        grid_spec=pltpu.PrefetchScalarGridSpec(
            num_scalar_prefetch=1,
            grid=(1,),
            in_specs=[whole(got.shape), pl.BlockSpec(memory_space=pl.ANY)],
            out_specs=pl.BlockSpec(memory_space=pl.ANY),
            scratch_shapes=[
                pltpu.VMEM(got.shape, jnp.float32),
                pltpu.SemaphoreType.DMA((got.shape[0] * PIECES,)),
            ],
        ),
        out_shape=jax.ShapeDtypeStruct(result.shape, jnp.float32),
        input_output_aliases={2: 0},
        cost_estimate=pl.CostEstimate(flops=0, bytes_accessed=got.size * 6, transcendentals=0),
        compiler_params=pltpu.CompilerParams(vmem_limit_bytes=PLACE_LIMIT << 20),
        name="place",
    )(where, got, result)


def open_kernel(vb, vir_hbm, occ_hbm, occ_out_hbm, out_hbm, vir_ref, occ_ref, in_sems, out_sems):
    aux = lax.axis_index("aux")
    parts = out_hbm.shape[1] // vb
    fetch_occ = pltpu.make_async_copy(occ_hbm, occ_ref, in_sems.at[parts])
    fetch_occ.start()
    fetches = []
    for j in range(parts):
        block = jnp.bitwise_xor(aux // 2, j) * 2 + aux % 2
        fetches.append(
            pltpu.make_async_copy(
                vir_hbm.at[:, pl.ds(pl.multiple_of(block * vb, vb), vb)], vir_ref.at[j], in_sems.at[j]
            )
        )
        fetches[-1].start()
    stores = [
        pltpu.make_async_copy(vir_ref.at[j], out_hbm.at[:, pl.ds(j * vb, vb)], out_sems.at[j])
        for j in range(parts)
    ]
    fetch_occ.wait()
    for g in range(occ_out_hbm.shape[0]):
        stores.append(pltpu.make_async_copy(occ_ref, occ_out_hbm.at[g], out_sems.at[parts + g]))
        stores[-1].start()
    for j in range(parts):
        fetches[j].wait()
        stores[j].start()
    for store in stores:
        store.wait()


def opening(vir, occ, group_size, aux, aux_size, vb):
    rows = vir.shape[0]
    parts = aux_size // 2
    copies = (group_size, *occ.shape)
    if vb % 128:
        order = jnp.bitwise_xor(aux // 2, jnp.arange(parts)) * 2 + aux % 2
        chosen = jnp.take(vir.reshape(rows, aux_size, vb), order, axis=1)
        return jnp.broadcast_to(occ[None], copies), chosen.reshape(rows, -1)
    anywhere = pl.BlockSpec(memory_space=pl.ANY)
    return pl.pallas_call(
        functools.partial(open_kernel, vb),
        in_specs=[anywhere] * 2,
        out_specs=[anywhere] * 2,
        scratch_shapes=[
            pltpu.VMEM((parts, rows, vb), vir.dtype),
            pltpu.VMEM(occ.shape, occ.dtype),
            pltpu.SemaphoreType.DMA((parts + 1,)),
            pltpu.SemaphoreType.DMA((parts + group_size,)),
        ],
        out_shape=[
            jax.ShapeDtypeStruct(copies, occ.dtype),
            jax.ShapeDtypeStruct((rows, parts * vb), vir.dtype),
        ],
        compiler_params=pltpu.CompilerParams(vmem_limit_bytes=63 << 20),
        name="opening",
    )(vir, occ)


def shards(integral_tiles, row_blocks, col_blocks, aux_blocks, tile_counts, occ_coeffs, vir_coeffs):
    group_size = lax.axis_size("grp")
    aux_size = lax.axis_size("aux")
    aux = lax.axis_index("aux")
    kmax, pb = integral_tiles.shape[2:4]
    orbitals = occ_coeffs.shape[0]
    virtuals = vir_coeffs.shape[1]
    vb = virtuals * orbitals // (group_size * aux_size)

    def swap(x, step):
        return lax.ppermute(x, "aux", [(a, a ^ step) for a in range(aux_size)])

    def hop(x, steps):
        return lax.ppermute(x, "grp", [(g, g ^ steps[g % 2]) for g in range(group_size)])

    occ, own = opening(vir_coeffs, occ_coeffs, group_size, aux, aux_size, vb)
    occ = lax.all_to_all(occ, "grp", split_axis=0, concat_axis=0, tiled=True)

    core = lax.axis_index("grp") % 2
    near = hop(own, (2, 4))
    far = hop(own, (4, 2))
    across = hop(near, (4, 2))
    halves = half_transform(
        integral_tiles[0, 0], row_blocks[0, 0], col_blocks[0, 0], aux_blocks[0, 0], tile_counts[0], occ
    )
    others = swap(halves, 1)
    halves, far, across = lax.optimization_barrier((halves, far, across))
    virs = [own, near, far, across]
    virs = virs + [hop(vir, (1, 1)) for vir in virs]

    halves = lax.all_to_all(halves, "grp", split_axis=0, concat_axis=0, tiled=True)
    others, halves = lax.optimization_barrier((others, halves))
    others = lax.all_to_all(others, "grp", split_axis=0, concat_axis=0, tiled=True)

    moved = [0, 2 + 2 * core, 4 - 2 * core, 6, 1, 5 - 2 * core, 3 + 2 * core, 7]
    moved = [jnp.bitwise_xor(lax.axis_index("grp"), step) for step in moved]
    where = jnp.stack([aux, jnp.bitwise_xor(aux, 1)] + moved).astype(jnp.int32)

    def trade(send):
        if aux_size == 4:
            return swap(send, 2)
        return jnp.stack([swap(send[j - 1], 2 * j) for j in range(1, aux_size // 2)])

    sizes = (kmax, pb, vb)
    columns = aux_size * PDEV
    if vb % 128:
        send_first, result = pair_transform("both", [halves], virs, where, *sizes, columns=columns)
        send_second, own_second = pair_transform("both", [others], virs, where, *sizes, columns=columns)
        got_first = trade(send_first)
        block = (jnp.bitwise_xor(aux, 1) * PDEV).astype(jnp.int32)
        own_second = lax.dynamic_slice_in_dim(own_second, (aux * PDEV).astype(jnp.int32), PDEV, 1)
        result = lax.dynamic_update_slice_in_dim(result, own_second, block, 1)
    else:
        (send_first,) = pair_transform("send", [halves], virs, where, *sizes)
        got_first = trade(send_first)
        others, _ = lax.optimization_barrier((others, send_first))
        (send_second,) = pair_transform("send", [others], virs, where, *sizes)
        others, halves, _ = lax.optimization_barrier((others, halves, send_second))
        (result,) = pair_transform("own", [halves], virs, where, *sizes, columns=columns)
        (result,) = pair_transform("own", [others], virs, where, *sizes, columns=columns, result=result)
    result = place(where, got_first, result, 0)
    return place(where, trade(send_second), result, 1)


def solution(mesh):
    in_specs = (
        P("grp", "aux", None, None, None, None),
        P("grp", "aux", None),
        P("grp", "aux", None),
        P("grp", "aux", None),
        P("grp", "aux"),
        P(None, "grp"),
        P("grp", None),
    )
    out_specs = P(("grp", "aux"), None)
    return jax.shard_map(shards, mesh=mesh, in_specs=in_specs, out_specs=out_specs, check_vma=False)
```
